256 devices in a mesh: dom: 64 (over x_hi, z, y), band: 4 (over x_lo, core).
Axes of the slice: x: 4 (x_hi: 2, x_lo: 2; x = x_hi * 2 + x_lo), y: 4, z: 8, core: 2. Of those that a mesh axis runs over, the one named last changes fastest.
Arguments:
- wavefn: bfloat16 [98304, 512], P('dom', 'band'), may hold values from -12 to 12
- cell_mats: bfloat16 [6144, 64, 64], P('dom'), may hold values from -0.18 to 2, as said below
- conn: int32 [6144, 64], P('dom'), may hold values from 0 to 2559, as said below
- proj: bfloat16 [128, 24, 18, 64], P('dom'), may hold values from -0.15625 to 0.15625
- coupling: float32 [128, 18, 18], P('dom'), may hold values from -3.2 to 0.6, as said below
- support: int32 [128, 24], replicated, may hold values from 0 to 6143, as said below
- bounds: float32 [3], replicated, may hold values from 1.4 to 21, as said below
- rotation: bfloat16 [512, 512], P(None, 'band'), may hold values from -0.25 to 0.25
Outputs:
- rotated: bfloat16 [98304, 512], P('dom', 'band')
The draws below stay inside these ranges and needn't reach their ends.
Inputs may be any that keep to these rules, and one draw needn't show every extreme that they name: conn[c, p] names node (d * 1536 + conn[c, p] - 512) mod 98304 of the periodic domain, d = c // 96; every node is named by exactly 4 entries of conn over all cells. Each atom's 24 cells are distinct; atom a is owned by dom index a // 2; of the 48 support cells of one owner's atoms at most 2 lie in the cells of any one dom index, and for every owner some dom index holds exactly 2. `cell_mats`: each cell matrix is symmetric. Each coupling matrix is symmetric. `bounds`: lower < cut < upper.
All inputs are finite; a program needn't handle non-finite values.
Results may differ from the reference program's by a relative error of at most 0.017.
Values may be sent and summed in bfloat16 or wider, within the bound.
No kernel may reach another device: no remote copies, remote signals or barrier semaphores. Data moves between devices by JAX's collectives and lax.ppermute only.
A program may use at most 64 MiB of HBM per device.

```python
import jax
import jax.numpy as jnp
from jax import lax

NVEC = 512
NPROJ = 18
CELLNODE = 64
CELL_DEV = 96
ATOM_DEV = 2
SUPP = 24
RIM = 512
DEG = 5
NODE_DEV = 1536
NODES = 98304
CELLS = 6144
ATOMS = 128
ENTRY = 48
CAP = 2
N_DOM = 64
N_BAND = 4


def permuted_pool(sub_key, pool):
    return pool[jax.random.permutation(sub_key, pool.shape[0])]


def draw_conn(key, part):
    key = jax.random.fold_in(key, 11)
    ext_index = jnp.arange(NODE_DEV + 2 * RIM, dtype=jnp.int32)
    own_index = ext_index - RIM
    interior = (own_index >= RIM) & (own_index < NODE_DEV - RIM)
    counts = jnp.where(interior, 4, 2).astype(jnp.int32)
    pool = jnp.repeat(ext_index, counts, total_repeat_length=4 * NODE_DEV)
    keys = jax.random.split(key, N_DOM)
    orders = jax.vmap(lambda sub_key: permuted_pool(sub_key, pool))(keys)
    return orders.reshape(CELLS, CELLNODE).astype(jnp.int32)


def support_rows(sub_key):
    pieces = jax.random.split(sub_key, 4)
    bins = N_DOM * CAP
    full_source = jax.random.randint(pieces[0], (), 0, N_DOM)
    ranks = jax.random.permutation(pieces[1], bins).astype(jnp.int32)
    bin_ids = jnp.arange(bins, dtype=jnp.int32)
    scores = ranks - bins * (bin_ids // CAP == full_source).astype(jnp.int32)
    chosen = jnp.argsort(scores, stable=True)[:ENTRY].astype(jnp.int32)
    chosen = chosen[jax.random.permutation(pieces[2], ENTRY)]
    source = chosen // CAP
    within = chosen % CAP
    offsets = jax.random.randint(pieces[3], (N_DOM,), 0, CELL_DEV).astype(jnp.int32)
    local_cell = (offsets[source] + within * (CELL_DEV // CAP)) % CELL_DEV
    return (source * CELL_DEV + local_cell).reshape(ATOM_DEV, SUPP).astype(jnp.int32)


def draw_support(key, part):
    key = jax.random.fold_in(key, 12)
    keys = jax.random.split(key, N_DOM)
    rows = jax.vmap(support_rows)(keys)
    return rows.reshape(ATOMS, SUPP).astype(jnp.int32)


def symmetric_matrix(key, count, order, spread, diag_vals):
    noise = jax.random.uniform(key, (count, order, order), jnp.float32, -spread, spread)
    sym_part = (noise + jnp.swapaxes(noise, 1, 2)) / 2
    rows = jnp.arange(order)
    on_diag = (rows[:, None] == rows[None, :]).astype(jnp.float32)
    return sym_part * (1 - on_diag) + diag_vals[:, :, None] * on_diag


def draw_cell_mats(key, part):
    key = jax.random.fold_in(key, 13)
    first, second = jax.random.split(key)
    diag_vals = jax.random.uniform(second, (CELLS, CELLNODE), jnp.float32, 1.0, 2.0)
    return symmetric_matrix(first, CELLS, CELLNODE, 0.18, diag_vals).astype(jnp.bfloat16)


def draw_coupling(key, part):
    key = jax.random.fold_in(key, 14)
    first, second = jax.random.split(key)
    unit = jax.random.uniform(second, (ATOMS, NPROJ), jnp.float32)
    diag_vals = -3.2 + 3.8 * unit
    return symmetric_matrix(first, ATOMS, NPROJ, 0.2, diag_vals)


def draw_bounds(key, part):
    key = jax.random.fold_in(key, 15)
    unit = jax.random.uniform(key, (3,), jnp.float32)
    return jnp.stack([1.4 + 0.6 * unit[0], 9.0 + 1.5 * unit[1], 18.0 + 3.0 * unit[2]]).astype(jnp.float32)


def block_scale(own_key, extent, cuts, low, top_value):
    def one(position, parts):
        heights = jax.random.uniform(jax.random.fold_in(jax.random.fold_in(own_key, 6), position), (parts,), jnp.float32, low / len(cuts), top_value / len(cuts))
        return jnp.repeat(jnp.exp(heights), extent[position] // parts).reshape((-1,) + (1,) * (len(extent) - position - 1))

    gain = one(*cuts[0])
    for cut in cuts[1:]:
        gain = gain * one(*cut)
    return gain


def scatter_about(rng, extent, deviation, bound, shards=(), kind=jnp.bfloat16):
    level = block_scale(rng, extent, shards, -0.22, 0.18) if shards else 1.0
    array = jax.random.normal(rng, extent, jnp.float32) * deviation * level
    return jnp.minimum(jnp.maximum(array, -bound), bound).astype(kind)


def setup_inputs(seed: int = 0) -> dict:
    streams_of = jax.random.split(jax.random.key(seed), 9)
    return {
        "wavefn": scatter_about(streams_of[0], (NODES, NVEC), 2.0, 12.0, ((0, 64), (1, 4))),
        "cell_mats": draw_cell_mats(jax.random.fold_in(streams_of[8], 71), 0),
        "conn": draw_conn(jax.random.fold_in(streams_of[8], 71), 0),
        "proj": scatter_about(streams_of[3], (ATOMS, SUPP, NPROJ, CELLNODE), (CELLNODE * SUPP) ** -0.5, 0.15625, ((0, 64),)),
        "coupling": draw_coupling(jax.random.fold_in(streams_of[8], 71), 0),
        "support": draw_support(jax.random.fold_in(streams_of[8], 71), 0),
        "bounds": draw_bounds(jax.random.fold_in(streams_of[8], 71), 0),
        "rotation": scatter_about(streams_of[7], (NVEC, NVEC), NVEC ** -0.5, 0.25, ((1, 4),)),
    }


def apply_operator(block, glob_conn, cell_mats, proj, coupling, support):
    cols = block.shape[1]
    cell_vals = block[glob_conn].astype(jnp.float32)
    local_term = jnp.einsum("cpq,cqv->cpv", cell_mats.astype(jnp.float32), cell_vals)
    entry_vals = cell_vals[support]
    proj_wide = proj.astype(jnp.float32)
    coeffs = jnp.einsum("aspn,asnv->apv", proj_wide, entry_vals)
    weights = jnp.einsum("apq,aqv->apv", coupling, coeffs, precision=lax.Precision.HIGHEST).astype(jnp.bfloat16)
    contrib = jnp.einsum("aspn,apv->asnv", proj_wide, weights.astype(jnp.float32)).astype(jnp.bfloat16)
    projector_term = jnp.zeros_like(local_term).at[support.reshape(-1)].add(
        contrib.reshape(-1, CELLNODE, cols).astype(jnp.float32))
    cell_total = local_term + projector_term
    return jnp.zeros((NODES, cols), jnp.float32).at[glob_conn.reshape(-1)].add(cell_total.reshape(-1, cols))


def filtered(block, glob_conn, cell_mats, proj, coupling, support, bounds):
    lower, cut, upper = bounds[0], bounds[1], bounds[2]
    half_width = (upper - cut) / 2
    center = (upper + cut) / 2
    sigma_first = half_width / (lower - center)
    sigma_now = sigma_first
    previous = block
    image = apply_operator(previous, glob_conn, cell_mats, proj, coupling, support)
    current = ((sigma_first / half_width) * (image - center * previous.astype(jnp.float32))).astype(jnp.bfloat16)
    for turn_index in range(DEG - 1):
        sigma_next = 1 / (2 / sigma_first - sigma_now)
        image = apply_operator(current, glob_conn, cell_mats, proj, coupling, support)
        upcoming = (2 * sigma_next / half_width) * (image - center * current.astype(jnp.float32))
        upcoming = (upcoming - (sigma_now * sigma_next) * previous.astype(jnp.float32)).astype(jnp.bfloat16)
        previous, current, sigma_now = current, upcoming, sigma_next
    return current


def reference(wavefn, cell_mats, conn, proj, coupling, support, bounds, rotation):
    block_cols = NVEC // N_BAND
    cell_owner = jnp.arange(CELLS, dtype=jnp.int32) // CELL_DEV
    glob_conn = ((cell_owner * NODE_DEV)[:, None] + conn - RIM) % NODES
    glob_conn = glob_conn.astype(jnp.int32)
    blocks = wavefn.reshape(NODES, N_BAND, block_cols).transpose(1, 0, 2)

    def one_block(block):
        return filtered(block, glob_conn, cell_mats, proj, coupling, support, bounds)

    done = lax.map(one_block, blocks)
    whole = done.transpose(1, 0, 2).reshape(NODES, NVEC)
    rotated = jnp.dot(whole.astype(jnp.float32), rotation.astype(jnp.float32).T,
                      precision=lax.Precision.HIGHEST, preferred_element_type=jnp.float32)
    return rotated.astype(jnp.bfloat16)
```

```python
import jax
import jax.numpy as jnp
from jax import lax
from jax.experimental import pallas as pl
from jax.experimental.pallas import tpu as pltpu
from jax.sharding import PartitionSpec as P

RIM = 512
DEG = 5
ROWS = 40
LO = 256
STEP_CELLS = 32
MIB = 1024 * 1024

BF16 = jnp.bfloat16
F32 = jnp.float32


def params(mib, *semantics):
    return pltpu.CompilerParams(dimension_semantics=semantics, vmem_limit_bytes=mib * MIB)


def dot(a, b, a_dim, b_dim, **kw):
    return lax.dot_general(
        a, b, (((a_dim,), (b_dim,)), ((), ())), preferred_element_type=F32, **kw
    )


def joined_kernel(cells, out):
    order = cells.shape[1]
    out[...] = jnp.zeros_like(out)
    for group in range(out.shape[0]):
        for i in range(out.shape[1] // order):
            part = pl.ds(i * order, order)
            out[group, part, part] = cells[group * (out.shape[1] // order) + i]


def joined(cell_mats, join, steps):
    cell_count, order, _ = cell_mats.shape
    groups = cell_count // join // steps
    return pl.pallas_call(
        joined_kernel,
        grid=(steps,),
        in_specs=[pl.BlockSpec((groups * join, order, order), lambda s: (s, 0, 0))],
        out_specs=pl.BlockSpec((groups, join * order, join * order), lambda s: (s, 0, 0)),
        out_shape=jax.ShapeDtypeStruct(
            (cell_count // join, join * order, join * order), BF16
        ),
        compiler_params=params(12, "arbitrary"),
        name="joined",
    )(cell_mats)


def local_kernel(state, conn, mats, image, to_previous, to_next, packed, total):
    step = pl.program_id(0)
    cols = state.shape[0]
    half = packed.shape[1]

    @pl.when(step == 0)
    def _():
        packed[:cols] = state[:, :half]
        packed[cols:] = state[:, half:]

    index = conn[0]
    entries = index.shape[1]
    upper = index >= half
    within = jnp.where(upper, index - half, index).astype(jnp.int16)
    row = lax.broadcasted_iota(jnp.int16, (half, entries), 0)
    hot = jnp.where(row == within, BF16(1.0), BF16(0.0))
    both = dot(packed[...], hot, 1, 0)
    vals = jnp.where(upper, both[cols:], both[:cols]).astype(BF16)
    width = mats.shape[1]
    term = jnp.concatenate(
        [
            dot(vals[:, i * width : (i + 1) * width], mats[i], 1, 1)
            for i in range(entries // width)
        ],
        axis=1,
    )
    spread = jnp.concatenate(
        [jnp.where(upper, 0.0, term), jnp.where(upper, term, 0.0)], axis=0
    ).astype(BF16)
    part = dot(spread, hot, 1, 1)

    @pl.when(step == 0)
    def _():
        total[...] = part

    @pl.when(step > 0)
    def _():
        total[...] += part

    @pl.when(step == pl.num_programs(0) - 1)
    def _():
        image[:, :half] = total[:cols]
        image[:, half:] = total[cols:]
        to_previous[...] = total[:cols, : 2 * RIM].astype(BF16)
        to_next[...] = total[cols:, half - 2 * RIM :].astype(BF16)


def local_part(state, conn_rows, mats):
    cols, ext_count = state.shape
    steps, _, entries = conn_rows.shape
    half = ext_count // 2
    groups = mats.shape[0] // steps
    width = mats.shape[1]
    whole = lambda s: (0, 0)
    shared = jax.ShapeDtypeStruct((cols, 2 * RIM), BF16)
    return pl.pallas_call(
        local_kernel,
        grid=(steps,),
        in_specs=[
            pl.BlockSpec((cols, ext_count), whole),
            pl.BlockSpec((1, 1, entries), lambda s: (s, 0, 0)),
            pl.BlockSpec((groups, width, width), lambda s: (s, 0, 0)),
        ],
        out_specs=[
            pl.BlockSpec((cols, ext_count), whole),
            pl.BlockSpec((cols, 2 * RIM), whole),
            pl.BlockSpec((cols, 2 * RIM), whole),
        ],
        out_shape=[jax.ShapeDtypeStruct((cols, ext_count), F32), shared, shared],
        scratch_shapes=[
            pltpu.VMEM((2 * cols, half), BF16),
            pltpu.VMEM((2 * cols, half), F32),
        ],
        compiler_params=params(56, "arbitrary"),
        cost_estimate=pl.CostEstimate(
            flops=2 * 2 * steps * entries * half * 2 * cols,
            bytes_accessed=6 * MIB,
            transcendentals=0,
        ),
        name="local_part",
    )(state, conn_rows, mats)


def sort_out_kernel(entry_of, proj, out):
    dom_count = out.shape[0]
    cap = entry_of.shape[0] // dom_count

    def one(slot):
        entry = entry_of[slot]
        share = jnp.where(entry >= 0, 1.0, 0.0)
        return proj[jnp.maximum(entry, 0)].astype(F32) * share

    @pl.loop(0, dom_count, unroll=8)
    def _(dom):
        out[dom] = jnp.concatenate(
            [one(dom * cap + j) for j in range(cap)], axis=1
        ).astype(BF16)


def sort_out(entry_of, proj, dom_count):
    entry_count, proj_count, cell_nodes = proj.shape
    cap = entry_of.shape[0] // dom_count
    return pl.pallas_call(
        sort_out_kernel,
        in_specs=[
            pl.BlockSpec(memory_space=pltpu.SMEM),
            pl.BlockSpec(memory_space=pltpu.VMEM),
        ],
        out_specs=pl.BlockSpec(memory_space=pltpu.VMEM),
        out_shape=jax.ShapeDtypeStruct((dom_count, proj_count, cap * cell_nodes), BF16),
        compiler_params=params(8),
        name="sort_out",
    )(entry_of, proj)


def assemble_kernel(low, here, high, atom_row, high_part, low_part, now, out, coeffs):
    owners, proj_count, _ = here.shape
    blocks = out.shape[1] // LO
    atoms = 2
    pieces = []
    for i in range(owners):
        rows = jnp.concatenate([low[i], here[i], high[i]], axis=1).astype(F32)
        entries = rows.shape[1]
        atom = atom_row[i]
        parts = [jnp.where(atom == a, rows, 0.0) for a in range(atoms)]
        parts.append(jnp.zeros((ROWS - atoms * proj_count, entries), F32))
        rows = jnp.concatenate(parts, axis=0)
        high_row = high_part[i]
        spread = jnp.concatenate(
            [jnp.where(high_row == h, rows, 0.0) for h in range(blocks)], axis=0
        ).astype(BF16)
        row = lax.broadcasted_iota(jnp.int16, (LO, entries), 0)
        hot = jnp.where(row == low_part[i].astype(jnp.int16), BF16(1.0), BF16(0.0))
        pieces.append(dot(spread, hot, 1, 1))
    for h in range(blocks):
        out[:, h * LO : (h + 1) * LO] = jnp.concatenate(
            [piece[h * ROWS : (h + 1) * ROWS] for piece in pieces], axis=0
        ).astype(BF16)
    inside = out[:, RIM : RIM + now.shape[1]]
    coeffs[...] = dot(inside, now[...], 1, 1).astype(BF16)


def assemble(low, here, high, atom_row, high_part, low_part, now):
    owner_count, proj_count, lanes = here.shape
    entries = atom_row.shape[2]
    cols, node_count = now.shape
    group = 8
    values = pl.BlockSpec((group, proj_count, lanes), lambda s: (s, 0, 0))
    index = pl.BlockSpec((group, 1, entries), lambda s: (s, 0, 0))
    return pl.pallas_call(
        assemble_kernel,
        grid=(owner_count // group,),
        in_specs=[values] * 3 + [index] * 3 + [pl.BlockSpec((cols, node_count), lambda s: (0, 0))],
        out_specs=[
            pl.BlockSpec((group * ROWS, node_count + 2 * RIM), lambda s: (s, 0)),
            pl.BlockSpec((group * ROWS, cols), lambda s: (s, 0)),
        ],
        out_shape=[
            jax.ShapeDtypeStruct((owner_count * ROWS, node_count + 2 * RIM), BF16),
            jax.ShapeDtypeStruct((owner_count * ROWS, cols), BF16),
        ],
        compiler_params=params(56, "arbitrary"),
        cost_estimate=pl.CostEstimate(
            flops=2 * owner_count * ROWS * node_count * (entries + cols),
            bytes_accessed=16 * MIB,
            transcendentals=0,
        ),
        name="assemble",
    )(low, here, high, atom_row, high_part, low_part, now)


def begin_kernel(scal, table, weights, now, before, image, part, out, total, flipped):
    step = pl.program_id(0)
    last = pl.num_programs(0) - 1
    edge = (step == 0) | (step == last)

    def add(value):
        return dot(table[...], value.astype(BF16), 1, 1)

    @pl.when(step == 0)
    def _():
        flipped[...] = weights[...].T
        total[...] = add(scal[0] * image[...])

    @pl.when(jnp.logical_not(edge))
    def _():
        value = scal[0] * (
            image[...] + dot(flipped[...], table[...], 1, 0) - scal[1] * now[...].astype(F32)
        )
        value -= scal[2] * before[...].astype(F32)
        part[...] = value
        total[...] += add(value)

    @pl.when(step == last)
    def _():
        out[...] = (total[...] + add(scal[0] * image[...])).astype(BF16)


def begin(scal, table, weights, now, before, image):
    rows, ext_count = table.shape
    cols = now.shape[0]
    steps = ext_count // RIM
    block = pl.BlockSpec((cols, RIM), lambda h: (0, h))
    inside = pl.BlockSpec((cols, RIM), lambda h: (0, jnp.clip(h - 1, 0, steps - 3)))
    whole = pl.BlockSpec((rows, cols), lambda h: (0, 0))
    return pl.pallas_call(
        begin_kernel,
        grid=(steps,),
        in_specs=[
            pl.BlockSpec(memory_space=pltpu.SMEM),
            pl.BlockSpec((rows, RIM), lambda h: (0, h)),
            whole,
            block,
            block,
            block,
        ],
        out_specs=[inside, whole],
        out_shape=[
            jax.ShapeDtypeStruct((cols, ext_count - 2 * RIM), F32),
            jax.ShapeDtypeStruct((rows, cols), BF16),
        ],
        scratch_shapes=[pltpu.VMEM((rows, cols), F32), pltpu.VMEM((cols, rows), BF16)],
        compiler_params=params(56, "arbitrary"),
        cost_estimate=pl.CostEstimate(
            flops=4 * rows * ext_count * cols,
            bytes_accessed=18 * MIB,
            transcendentals=0,
        ),
        name="begin",
    )(scal, table, weights, now, before, image)


def finish_kernel(
    scal, table, weights, now, before, image, part, from_previous, from_next, new
):
    step = pl.program_id(0)
    last = pl.num_programs(0) - 1
    edge = (step == 0) | (step == last)
    came = jnp.where(step <= 1, from_previous[...], from_next[...]).astype(F32)
    came *= jnp.where((step <= 1) | (step >= last - 1), 1.0, 0.0)

    @pl.when(edge)
    def _():
        value = image[...] + came + dot(weights[...].T, table[...], 1, 0)
        value = scal[0] * (value - scal[1] * now[...].astype(F32))
        new[...] = (value - scal[2] * before[...].astype(F32)).astype(BF16)

    @pl.when(jnp.logical_not(edge))
    def _():
        new[...] = (part[...] + scal[0] * came).astype(BF16)


def finish(scal, table, weights, now, before, image, part, from_previous, from_next):
    rows, ext_count = table.shape
    cols = now.shape[0]
    steps = ext_count // RIM
    block = pl.BlockSpec((cols, RIM), lambda h: (0, h))

    def ends(h):
        return (0, jnp.where(h < steps - 2, 0, steps - 1))

    return pl.pallas_call(
        finish_kernel,
        grid=(steps,),
        in_specs=[
            pl.BlockSpec(memory_space=pltpu.SMEM),
            pl.BlockSpec((rows, RIM), ends),
            pl.BlockSpec((rows, cols), lambda h: (0, 0)),
            pl.BlockSpec((cols, RIM), ends),
            pl.BlockSpec((cols, RIM), ends),
            pl.BlockSpec((cols, RIM), ends),
            pl.BlockSpec((cols, RIM), lambda h: (0, jnp.clip(h - 1, 0, steps - 3))),
            pl.BlockSpec((cols, RIM), lambda h: (0, jnp.minimum(h, 1))),
            pl.BlockSpec((cols, RIM), lambda h: (0, jnp.where(h == steps - 1, 1, 0))),
        ],
        out_specs=block,
        out_shape=jax.ShapeDtypeStruct((cols, ext_count), BF16),
        compiler_params=params(56, "arbitrary"),
        cost_estimate=pl.CostEstimate(
            flops=4 * rows * RIM * cols, bytes_accessed=10 * MIB, transcendentals=0
        ),
        name="finish",
    )(scal, table, weights, now, before, image, part, from_previous, from_next)


def final_kernel(
    scal, table, weights, now, before, image, from_previous, from_next, new, flipped
):
    step = pl.program_id(0)
    last = pl.num_programs(0) - 1

    @pl.when(step == 0)
    def _():
        flipped[...] = weights[...].T

    value = image[...] + dot(flipped[...], table[...], 1, 0)
    value += jnp.where(step == 0, 1.0, 0.0) * from_previous[...].astype(F32)
    value += jnp.where(step == last, 1.0, 0.0) * from_next[...].astype(F32)
    value = scal[0] * (value - scal[1] * now[...].astype(F32))
    new[...] = (value - scal[2] * before[...].astype(F32)).astype(BF16)


def final_turn(scal, table, weights, now, before, image, from_previous, from_next):
    rows, ext_count = table.shape
    cols = now.shape[0]
    steps = ext_count // RIM - 2
    inside = pl.BlockSpec((cols, RIM), lambda h: (0, h + 1))
    return pl.pallas_call(
        final_kernel,
        grid=(steps,),
        in_specs=[
            pl.BlockSpec(memory_space=pltpu.SMEM),
            pl.BlockSpec((rows, RIM), lambda h: (0, h + 1)),
            pl.BlockSpec((rows, cols), lambda h: (0, 0)),
            inside,
            inside,
            inside,
            pl.BlockSpec((cols, RIM), lambda h: (0, 1)),
            pl.BlockSpec((cols, RIM), lambda h: (0, 0)),
        ],
        out_specs=pl.BlockSpec((cols, RIM), lambda h: (0, h)),
        out_shape=jax.ShapeDtypeStruct((cols, ext_count - 2 * RIM), BF16),
        scratch_shapes=[pltpu.VMEM((cols, rows), BF16)],
        compiler_params=params(56, "arbitrary"),
        cost_estimate=pl.CostEstimate(
            flops=2 * rows * ext_count * cols, bytes_accessed=11 * MIB, transcendentals=0
        ),
        name="final_turn",
    )(scal, table, weights, now, before, image, from_previous, from_next)


def rotate_kernel(first, second, third, fourth, mats, out):
    total = dot(first[...], mats[0], 0, 1)
    for i, piece in enumerate((second, third, fourth)):
        total += dot(piece[...], mats[i + 1], 0, 1)
    out[...] = total.astype(BF16)


def rotate(pieces, mats):
    cols, node_count = pieces[0].shape
    step = RIM
    block = pl.BlockSpec((cols, step), lambda h: (0, h))
    return pl.pallas_call(
        rotate_kernel,
        grid=(node_count // step,),
        in_specs=[block] * 4 + [pl.BlockSpec(mats.shape, lambda h: (0, 0, 0))],
        out_specs=pl.BlockSpec((step, cols), lambda h: (h, 0)),
        out_shape=jax.ShapeDtypeStruct((node_count, cols), BF16),
        compiler_params=params(12, "arbitrary"),
        name="rotate",
    )(*pieces, mats)


def couple_kernel(parts, coupling, out):
    coeffs = jnp.sum(parts[...].astype(F32), axis=0)
    weights = dot(coupling[...], coeffs, 1, 0, precision=lax.Precision.HIGHEST)
    out[...] = jnp.broadcast_to(weights.astype(BF16)[None], out.shape)


def couple(parts, coupling):
    return pl.pallas_call(
        couple_kernel,
        out_shape=jax.ShapeDtypeStruct(parts.shape, BF16),
        compiler_params=params(10),
        name="couple",
    )(parts, coupling)


def ring(count):
    forward = [(i, (i + 1) % count) for i in range(count)]
    return forward, [(target, source) for source, target in forward]


def body(wavefn, cell_mats, conn, proj, coupling, support, bounds, rotation):
    my_dom = lax.axis_index("dom")
    dom_count = lax.axis_size("dom")
    node_count, vec_cols = wavefn.shape
    cell_count, cell_nodes = conn.shape
    atom_count, supp_count, proj_count, _ = proj.shape
    entry_count = atom_count * supp_count
    slot_cap = 2
    slot_count = dom_count * slot_cap
    blocks = node_count // LO
    forward, backward = ring(dom_count)

    def exchange(to_next, to_previous):
        return (
            lax.ppermute(to_next, "dom", forward),
            lax.ppermute(to_previous, "dom", backward),
        )

    all_entries = support.reshape(dom_count, entry_count)
    entry_source = all_entries // cell_count
    entry_cell = all_entries % cell_count
    entry_atom = jnp.arange(entry_count, dtype=jnp.int32) // supp_count

    def slots_of(dom):
        here = (entry_source == dom).astype(jnp.int32)
        rank = jnp.cumsum(here, axis=1) - 1
        hit = here[:, :, None] * (
            rank[:, :, None] == jnp.arange(slot_cap, dtype=jnp.int32)
        ).astype(jnp.int32)
        cell = jnp.sum(hit * entry_cell[:, :, None], axis=1)
        atom = jnp.sum(hit * entry_atom[None, :, None], axis=1)
        return cell, atom

    offsets = (-1, 0, 1)
    slots = [slots_of((my_dom + offset) % dom_count) for offset in offsets]
    own_entries = lax.dynamic_slice_in_dim(all_entries, my_dom, 1, 0)[0]
    own_source = own_entries // cell_count
    positions = jnp.arange(entry_count, dtype=jnp.int32)
    earlier = (own_source[:, None] == own_source[None, :]) & (
        positions[None, :] < positions[:, None]
    )
    own_slot = own_source * slot_cap + jnp.sum(earlier.astype(jnp.int32), axis=1)

    slot_ids = jnp.arange(slot_count, dtype=jnp.int32)
    place = (slot_ids[:, None] == own_slot[None, :]).astype(jnp.int32)
    entry_of = jnp.sum(place * (positions[None, :] + 1), axis=1) - 1
    outgoing = sort_out(entry_of, proj.reshape(entry_count, proj_count, cell_nodes), dom_count)
    here = lax.all_to_all(outgoing, "dom", split_axis=0, concat_axis=0, tiled=True)
    conn_low, conn_high = exchange(conn, conn)
    own = wavefn.T

    conn_rows = conn.reshape(cell_count // STEP_CELLS, 1, STEP_CELLS * cell_nodes)
    mats = joined(cell_mats, 4, cell_count // STEP_CELLS)

    def local(state):
        image, to_previous, to_next = local_part(state, conn_rows, mats)
        return (image, *exchange(to_next, to_previous))

    low, high = exchange(own[:, node_count - RIM :], own[:, :RIM])
    current = jnp.concatenate([low, own, high], axis=1)
    image, from_previous, from_next = local(current)
    here, image = lax.optimization_barrier((here, image))
    values_low, values_high = exchange(here, here)
    node_rows, atom_rows = [], []
    for offset, cells, (cell, atom) in zip(offsets, (conn_low, conn, conn_high), slots):
        node = cells[cell] + offset * node_count
        node_rows.append(node)
        atom_rows.append(jnp.broadcast_to(atom[:, :, None], node.shape))
    node_row = jnp.stack(node_rows, axis=1).reshape(dom_count, 1, -1)
    atom_row = jnp.stack(atom_rows, axis=1).reshape(dom_count, 1, -1)
    inside = (node_row >= 0) & (node_row < node_count + 2 * RIM)
    high_part = jnp.where(inside, node_row // LO, -1)
    low_part = jnp.where(inside, node_row % LO, 0)
    table, coeffs = assemble(values_low, here, values_high, atom_row, high_part, low_part, own)

    pair = jnp.zeros((ROWS, ROWS), F32)
    for a in range(atom_count):
        pair = lax.dynamic_update_slice(pair, coupling[a], (a * proj_count, a * proj_count))

    me = lax.axis_index("band")
    rotation_pieces = rotation.reshape(-1, vec_cols, vec_cols)
    swaps = [[(i, i ^ k) for i in range(4)] for k in range(4)]

    def rows_for(band):
        return lax.dynamic_index_in_dim(rotation_pieces, band, 0, keepdims=False)

    rotation_rows = [rows_for(me)]
    for k in range(1, 4):
        rotation_rows.append(lax.ppermute(rows_for(me ^ k), "band", swaps[k]))
    rotation_rows = jnp.stack(rotation_rows)

    def swap(block):
        return lax.all_to_all(block, "dom", split_axis=0, concat_axis=0, tiled=True)

    lower, cut, upper = (bounds[0], bounds[1], bounds[2])
    half_width = (upper - cut) / 2
    center = (upper + cut) / 2
    sigma_first = half_width / (lower - center)
    sigma_now = sigma_first

    previous = current
    scal = jnp.stack([sigma_first / half_width, center, jnp.zeros_like(center)])
    for turn_index in range(DEG):
        last = turn_index == DEG - 1
        arrived = swap(coeffs.reshape(dom_count, ROWS, vec_cols))
        if turn_index:
            current, previous = finish(*begun, from_previous, from_next), current
            if last:
                image, from_previous, from_next = local(current)
                arrived, image = lax.optimization_barrier((arrived, image))
        coupled = couple(arrived, pair)
        if not last:
            coupled, current, rotation_rows = lax.optimization_barrier(
                (coupled, current, rotation_rows)
            )
            if turn_index:
                image, from_previous, from_next = local(current)
        weights = swap(coupled).reshape(dom_count * ROWS, vec_cols)
        args = (scal, table, weights, current, previous, image)
        if last:
            done = final_turn(*args, from_previous, from_next)
        else:
            part, coeffs = begin(*args)
            begun = (*args, part)
            coeffs, from_previous, from_next = lax.optimization_barrier(
                (coeffs, from_previous, from_next)
            )
        sigma_next = 1 / (2 / sigma_first - sigma_now)
        scal = jnp.stack([2 * sigma_next / half_width, center, sigma_now * sigma_next])
        sigma_now = sigma_next

    beside = lax.ppermute(done, "band", swaps[1])
    across = lax.ppermute(done, "band", swaps[2])
    last = lax.ppermute(across, "band", swaps[1])
    return rotate((done, beside, across, last), rotation_rows)


def solution(mesh):
    in_specs = (
        P("dom", "band"),
        P("dom", None, None),
        P("dom", None),
        P("dom", None, None, None),
        P("dom", None, None),
        P(),
        P(),
        P(None, "band"),
    )
    out_specs = P("dom", "band")
    return jax.shard_map(body, mesh=mesh, in_specs=in_specs, out_specs=out_specs, check_vma=False)
```

```python
import jax
import jax.numpy as jnp
from jax import lax
from jax.experimental import pallas as pl
from jax.experimental.pallas import tpu as pltpu
from jax.sharding import PartitionSpec as P

RIM = 512
DEG = 5
PADDED = 40
LO = 256
STEP_CELLS = 32
MIB = 1024 * 1024

BF16 = jnp.bfloat16
F32 = jnp.float32


def params(mib, *semantics):
    return pltpu.CompilerParams(dimension_semantics=semantics, vmem_limit_bytes=mib * MIB)


def dot(a, b, a_dim, b_dim, **kw):
    return lax.dot_general(
        a, b, (((a_dim,), (b_dim,)), ((), ())), preferred_element_type=F32, **kw
    )


def joined_kernel(cells, out):
    order = cells.shape[1]
    out[...] = jnp.zeros_like(out)
    for group in range(out.shape[0]):
        for i in range(out.shape[1] // order):
            part = pl.ds(i * order, order)
            out[group, part, part] = cells[group * (out.shape[1] // order) + i]


def joined(cell_mats, join, steps):
    cell_count, order, _ = cell_mats.shape
    groups = cell_count // join // steps
    return pl.pallas_call(
        joined_kernel,
        grid=(steps,),
        in_specs=[pl.BlockSpec((groups * join, order, order), lambda s: (s, 0, 0))],
        out_specs=pl.BlockSpec((groups, join * order, join * order), lambda s: (s, 0, 0)),
        out_shape=jax.ShapeDtypeStruct(
            (cell_count // join, join * order, join * order), BF16
        ),
        compiler_params=params(56, "arbitrary"),
        name="joined",
    )(cell_mats)


def local_kernel(side, state, conn, mats, image, first, second, packed, total):
    step = pl.program_id(0)
    cols = state.shape[0]
    half = packed.shape[1]

    @pl.when(step == 0)
    def _():
        packed[:cols] = state[:, :half]
        packed[cols:] = state[:, half:]

    index = conn[0]
    entries = index.shape[1]
    upper = index >= half
    within = jnp.where(upper, index - half, index).astype(jnp.int16)
    row = lax.broadcasted_iota(jnp.int16, (half, entries), 0)
    hot = jnp.where(row == within, BF16(1.0), BF16(0.0))
    both = dot(packed[...], hot, 1, 0)
    vals = jnp.where(upper, both[cols:], both[:cols]).astype(BF16)
    width = mats.shape[1]
    term = jnp.concatenate(
        [
            dot(vals[:, i * width : (i + 1) * width], mats[i], 1, 1)
            for i in range(entries // width)
        ],
        axis=1,
    )
    spread = jnp.concatenate(
        [jnp.where(upper, 0.0, term), jnp.where(upper, term, 0.0)], axis=0
    ).astype(BF16)
    part = dot(spread, hot, 1, 1)

    @pl.when(step == 0)
    def _():
        total[...] = part

    @pl.when(step > 0)
    def _():
        total[...] += part

    @pl.when(step == pl.num_programs(0) - 1)
    def _():
        image[:, :half] = total[:cols]
        image[:, half:] = total[cols:]
        to_previous = total[:cols, : 2 * RIM].astype(BF16)
        to_next = total[cols:, half - 2 * RIM :].astype(BF16)
        even = side[0] == 0
        first[...] = jnp.where(even, to_next, to_previous)
        second[...] = jnp.where(even, to_previous, to_next)


def local_part(side, state, conn_rows, mats):
    cols, ext_count = state.shape
    steps, _, entries = conn_rows.shape
    half = ext_count // 2
    groups = mats.shape[0] // steps
    width = mats.shape[1]
    whole = lambda s: (0, 0)
    shared = jax.ShapeDtypeStruct((cols, 2 * RIM), BF16)
    return pl.pallas_call(
        local_kernel,
        grid=(steps,),
        in_specs=[
            pl.BlockSpec(memory_space=pltpu.SMEM),
            pl.BlockSpec((cols, ext_count), whole),
            pl.BlockSpec((1, 1, entries), lambda s: (s, 0, 0)),
            pl.BlockSpec((groups, width, width), lambda s: (s, 0, 0)),
        ],
        out_specs=[
            pl.BlockSpec((cols, ext_count), whole),
            pl.BlockSpec((cols, 2 * RIM), whole),
            pl.BlockSpec((cols, 2 * RIM), whole),
        ],
        out_shape=[jax.ShapeDtypeStruct((cols, ext_count), F32), shared, shared],
        scratch_shapes=[
            pltpu.VMEM((2 * cols, half), BF16),
            pltpu.VMEM((2 * cols, half), F32),
        ],
        compiler_params=params(56, "arbitrary"),
        cost_estimate=pl.CostEstimate(
            flops=2 * 2 * steps * entries * half * 2 * cols,
            bytes_accessed=6 * MIB,
            transcendentals=0,
        ),
        name="local_part",
    )(side, state, conn_rows, mats)


def sort_out_kernel(entry_of, proj, out):
    dom_count = out.shape[0]
    cap = entry_of.shape[0] // dom_count

    def one(slot):
        entry = entry_of[slot]
        share = jnp.where(entry >= 0, 1.0, 0.0)
        return proj[jnp.maximum(entry, 0)].astype(F32) * share

    @pl.loop(0, dom_count, unroll=8)
    def _(dom):
        out[dom] = jnp.concatenate(
            [one(dom * cap + j) for j in range(cap)], axis=1
        ).astype(BF16)


def sort_out(entry_of, proj, dom_count):
    entry_count, proj_count, cell_nodes = proj.shape
    cap = entry_of.shape[0] // dom_count
    return pl.pallas_call(
        sort_out_kernel,
        in_specs=[
            pl.BlockSpec(memory_space=pltpu.SMEM),
            pl.BlockSpec(memory_space=pltpu.VMEM),
        ],
        out_specs=pl.BlockSpec(memory_space=pltpu.VMEM),
        out_shape=jax.ShapeDtypeStruct((dom_count, proj_count, cap * cell_nodes), BF16),
        compiler_params=params(8),
        name="sort_out",
    )(entry_of, proj)


def at_nodes(values, atom, high, low, blocks):
    proj_count, entries = values.shape
    atoms = 2
    parts = [jnp.where(atom == a, values, 0.0) for a in range(atoms)]
    parts.append(jnp.zeros((PADDED - atoms * proj_count, entries), F32))
    rows = jnp.concatenate(parts, axis=0)
    spread = jnp.concatenate([jnp.where(high == h, rows, 0.0) for h in blocks], axis=0)
    row = lax.broadcasted_iota(jnp.int16, (LO, entries), 0)
    hot = jnp.where(row == low.astype(jnp.int16), BF16(1.0), BF16(0.0))
    return dot(spread.astype(BF16), hot, 1, 1)


def block_rows(pieces, at, rows):
    return jnp.concatenate(
        [piece[at * PADDED : at * PADDED + rows] for piece in pieces], axis=0
    ).astype(BF16)


def split_owners(stacked, out):
    owners, rows, _ = out.shape
    for i in range(owners):
        out[i] = stacked[i * rows : (i + 1) * rows].astype(BF16)


def stack_owners(weights, stacked):
    owners, rows, _ = weights.shape
    for i in range(owners):
        stacked[i * rows : (i + 1) * rows] = weights[i].astype(F32)


def first_kernel(here, atom, high, low, now, coeffs, table, stacked):
    owners = here.shape[0]
    rows = coeffs.shape[1]
    blocks = range(now.shape[1] // LO)
    pieces = [
        at_nodes(here[i].astype(F32), atom[i], high[i], low[i], blocks) for i in range(owners)
    ]
    for h in blocks:
        table[:, h * LO : (h + 1) * LO] = block_rows(pieces, h, rows)
    stacked[...] = dot(table[...], now[...], 1, 1)
    split_owners(stacked, coeffs)


def first_coeffs(here, atom_row, high_part, low_part, now):
    owner_count, proj_count, lanes = here.shape
    cols, ext_count = now.shape
    rows = 2 * proj_count
    group = 32
    index = pl.BlockSpec((group, 1, lanes), lambda s: (s, 0, 1))
    return pl.pallas_call(
        first_kernel,
        grid=(owner_count // group,),
        in_specs=[
            pl.BlockSpec((group, proj_count, lanes), lambda s: (s, 0, 0)),
            index,
            index,
            index,
            pl.BlockSpec((cols, ext_count), lambda s: (0, 0)),
        ],
        out_specs=pl.BlockSpec((group, rows, cols), lambda s: (s, 0, 0)),
        out_shape=jax.ShapeDtypeStruct((owner_count, rows, cols), BF16),
        scratch_shapes=[
            pltpu.VMEM((group * rows, ext_count), BF16),
            pltpu.VMEM((group * rows, cols), F32),
        ],
        compiler_params=params(48, "arbitrary"),
        cost_estimate=pl.CostEstimate(
            flops=2 * owner_count * rows * ext_count * (lanes + cols),
            bytes_accessed=2 * MIB,
            transcendentals=0,
        ),
        name="first_coeffs",
    )(here, atom_row, high_part, low_part, now)


def assemble_kernel(low, here, high, atom_row, high_part, low_part, out):
    owners, _, lanes = here.shape
    rows = out.shape[0] // owners
    block_count = out.shape[1] // LO
    edge = 2 * RIM // LO
    sides = (
        (low, here, slice(0, 2 * lanes), range(block_count - edge)),
        (here, high, slice(lanes, 3 * lanes), range(block_count - edge, block_count)),
    )
    for left, right, part, blocks in sides:
        pieces = []
        for i in range(owners):
            values = jnp.concatenate([left[i], right[i]], axis=1).astype(F32)
            pieces.append(
                at_nodes(
                    values, atom_row[i][:, part], high_part[i][:, part], low_part[i][:, part], blocks
                )
            )
        for at, h in enumerate(blocks):
            out[:, h * LO : (h + 1) * LO] = block_rows(pieces, at, rows)


def assemble(low, here, high, atom_row, high_part, low_part, ext_count):
    owner_count, proj_count, lanes = here.shape
    entries = atom_row.shape[2]
    rows = 2 * proj_count
    group = 8
    values = pl.BlockSpec((group, proj_count, lanes), lambda s: (s, 0, 0))
    index = pl.BlockSpec((group, 1, entries), lambda s: (s, 0, 0))
    return pl.pallas_call(
        assemble_kernel,
        grid=(owner_count // group,),
        in_specs=[values] * 3 + [index] * 3,
        out_specs=pl.BlockSpec((group * rows, ext_count), lambda s: (s, 0)),
        out_shape=jax.ShapeDtypeStruct((owner_count * rows, ext_count), BF16),
        compiler_params=params(56, "arbitrary"),
        cost_estimate=pl.CostEstimate(
            flops=2 * owner_count * rows * ext_count * entries,
            bytes_accessed=16 * MIB,
            transcendentals=0,
        ),
        name="assemble",
    )(low, here, high, atom_row, high_part, low_part)


def begin_kernel(
    scal, table, weights, now, before, image, part, out, total, flipped
):
    step = pl.program_id(0)
    last = pl.num_programs(0) - 1
    edge = (step == 0) | (step == last)

    def add(value):
        return dot(table[...], value.astype(BF16), 1, 1)

    @pl.when(step == 0)
    def _():
        stack_owners(weights, total)
        flipped[...] = total[...].T.astype(BF16)
        total[...] = add(scal[0] * image[...])

    @pl.when(jnp.logical_not(edge))
    def _():
        value = scal[0] * (
            image[...] + dot(flipped[...], table[...], 1, 0) - scal[1] * now[...].astype(F32)
        )
        value -= scal[2] * before[...].astype(F32)
        part[...] = value
        total[...] += add(value)

    @pl.when(step == last)
    def _():
        total[...] += add(scal[0] * image[...])
        split_owners(total, out)


def begin(scal, table, weights, now, before, image):
    rows, ext_count = table.shape
    cols = now.shape[0]
    steps = ext_count // RIM
    block = pl.BlockSpec((cols, RIM), lambda h: (0, h))
    inside = pl.BlockSpec((cols, RIM), lambda h: (0, jnp.clip(h - 1, 0, steps - 3)))
    whole = pl.BlockSpec(weights.shape, lambda h: (0, 0, 0))
    return pl.pallas_call(
        begin_kernel,
        grid=(steps,),
        in_specs=[
            pl.BlockSpec(memory_space=pltpu.SMEM),
            pl.BlockSpec((rows, RIM), lambda h: (0, h)),
            whole,
            block,
            block,
            block,
        ],
        out_specs=[inside, whole],
        out_shape=[
            jax.ShapeDtypeStruct((cols, ext_count - 2 * RIM), F32),
            jax.ShapeDtypeStruct(weights.shape, BF16),
        ],
        scratch_shapes=[pltpu.VMEM((rows, cols), F32), pltpu.VMEM((cols, rows), BF16)],
        compiler_params=params(56, "arbitrary"),
        cost_estimate=pl.CostEstimate(
            flops=4 * rows * ext_count * cols,
            bytes_accessed=18 * MIB,
            transcendentals=0,
        ),
        name="begin",
    )(scal, table, weights, now, before, image)


def finish_kernel(
    scal, side, table, weights, now, before, image, part, first, second,
    new, stacked, flipped,
):
    step = pl.program_id(0)
    last = pl.num_programs(0) - 1
    edge = (step == 0) | (step == last)
    came = jnp.where((step <= 1) == (side[0] == 0), second[...], first[...]).astype(F32)
    came *= jnp.where((step <= 1) | (step >= last - 1), 1.0, 0.0)

    @pl.when(step == 0)
    def _():
        stack_owners(weights, stacked)
        flipped[...] = stacked[...].T.astype(BF16)

    @pl.when(edge)
    def _():
        value = image[...] + came + dot(flipped[...], table[...], 1, 0)
        value = scal[0] * (value - scal[1] * now[...].astype(F32))
        new[...] = (value - scal[2] * before[...].astype(F32)).astype(BF16)

    @pl.when(jnp.logical_not(edge))
    def _():
        new[...] = (part[...] + scal[0] * came).astype(BF16)


def finish(scal, side, table, weights, now, before, image, part, first, second):
    rows, ext_count = table.shape
    cols = now.shape[0]
    steps = ext_count // RIM
    block = pl.BlockSpec((cols, RIM), lambda h: (0, h))

    def ends(h):
        return (0, jnp.where(h < steps - 2, 0, steps - 1))

    def shared(h):
        return (0, jnp.where((h == 0) | (h == steps - 2), 0, 1))

    return pl.pallas_call(
        finish_kernel,
        grid=(steps,),
        in_specs=[
            pl.BlockSpec(memory_space=pltpu.SMEM),
            pl.BlockSpec(memory_space=pltpu.SMEM),
            pl.BlockSpec((rows, RIM), ends),
            pl.BlockSpec(weights.shape, lambda h: (0, 0, 0)),
            pl.BlockSpec((cols, RIM), ends),
            pl.BlockSpec((cols, RIM), ends),
            pl.BlockSpec((cols, RIM), ends),
            pl.BlockSpec((cols, RIM), lambda h: (0, jnp.clip(h - 1, 0, steps - 3))),
            pl.BlockSpec((cols, RIM), shared),
            pl.BlockSpec((cols, RIM), shared),
        ],
        out_specs=block,
        out_shape=jax.ShapeDtypeStruct((cols, ext_count), BF16),
        scratch_shapes=[pltpu.VMEM((rows, cols), F32), pltpu.VMEM((cols, rows), BF16)],
        compiler_params=params(56, "arbitrary"),
        cost_estimate=pl.CostEstimate(
            flops=4 * rows * RIM * cols, bytes_accessed=10 * MIB, transcendentals=0
        ),
        name="finish",
    )(scal, side, table, weights, now, before, image, part, first, second)


def final_kernel(scal, table, weights, now, before, image, part, stacked, flipped):
    step = pl.program_id(0)

    @pl.when(step == 0)
    def _():
        stack_owners(weights, stacked)
        flipped[...] = stacked[...].T.astype(BF16)

    value = image[...] + dot(flipped[...], table[...], 1, 0)
    value = scal[0] * (value - scal[1] * now[...].astype(F32))
    part[...] = value - scal[2] * before[...].astype(F32)


def final_turn(scal, table, weights, now, before, image):
    rows, ext_count = table.shape
    cols = now.shape[0]
    steps = ext_count // RIM - 2
    inside = pl.BlockSpec((cols, RIM), lambda h: (0, h + 1))
    return pl.pallas_call(
        final_kernel,
        grid=(steps,),
        in_specs=[
            pl.BlockSpec(memory_space=pltpu.SMEM),
            pl.BlockSpec((rows, RIM), lambda h: (0, h + 1)),
            pl.BlockSpec(weights.shape, lambda h: (0, 0, 0)),
            inside,
            inside,
            inside,
        ],
        out_specs=pl.BlockSpec((cols, RIM), lambda h: (0, h)),
        out_shape=jax.ShapeDtypeStruct((cols, ext_count - 2 * RIM), F32),
        scratch_shapes=[pltpu.VMEM((rows, cols), F32), pltpu.VMEM((cols, rows), BF16)],
        compiler_params=params(56, "arbitrary"),
        cost_estimate=pl.CostEstimate(
            flops=2 * rows * ext_count * cols, bytes_accessed=11 * MIB, transcendentals=0
        ),
        name="final_turn",
    )(scal, table, weights, now, before, image)


def settle_kernel(scal, side, part, first, second, new):
    even = side[0] == 0
    from_previous = jnp.where(even, second[:, RIM:], first[:, RIM:]).astype(F32)
    from_next = jnp.where(even, first[:, :RIM], second[:, :RIM]).astype(F32)
    end = part.shape[1] - RIM
    new[:, :RIM] = (part[:, :RIM] + scal[0] * from_previous).astype(BF16)
    new[:, RIM:end] = part[:, RIM:end].astype(BF16)
    new[:, end:] = (part[:, end:] + scal[0] * from_next).astype(BF16)


def settle(scal, side, part, first, second):
    smem = pl.BlockSpec(memory_space=pltpu.SMEM)
    vmem = pl.BlockSpec(memory_space=pltpu.VMEM)
    return pl.pallas_call(
        settle_kernel,
        in_specs=[smem, smem, vmem, vmem, vmem],
        out_specs=vmem,
        out_shape=jax.ShapeDtypeStruct(part.shape, BF16),
        compiler_params=params(8),
        name="settle",
    )(scal, side, part, first, second)


def rotate_kernel(first, second, third, fourth, mats, out):
    total = dot(first[...], mats[0], 0, 1)
    for i, piece in enumerate((second, third, fourth)):
        total += dot(piece[...], mats[i + 1], 0, 1)
    out[...] = total.astype(BF16)


def rotate(pieces, mats):
    cols, node_count = pieces[0].shape
    step = RIM
    block = pl.BlockSpec((cols, step), lambda h: (0, h))
    return pl.pallas_call(
        rotate_kernel,
        grid=(node_count // step,),
        in_specs=[block] * 4 + [pl.BlockSpec(mats.shape, lambda h: (0, 0, 0))],
        out_specs=pl.BlockSpec((step, cols), lambda h: (h, 0)),
        out_shape=jax.ShapeDtypeStruct((node_count, cols), BF16),
        compiler_params=params(12, "arbitrary"),
        name="rotate",
    )(*pieces, mats)


def couple_kernel(parts, coupling, out):
    coeffs = jnp.sum(parts[...].astype(F32), axis=0)
    weights = dot(coupling[...], coeffs, 1, 0, precision=lax.Precision.HIGHEST)
    out[...] = jnp.broadcast_to(weights.astype(BF16)[None], out.shape)


def couple(parts, coupling):
    return pl.pallas_call(
        couple_kernel,
        out_shape=jax.ShapeDtypeStruct(parts.shape, BF16),
        compiler_params=params(10),
        name="couple",
    )(parts, coupling)


def pairs(count):
    first = [(i, i ^ 1) for i in range(count)]
    second = [(i, (i + 1 if i % 2 else i - 1) % count) for i in range(count)]
    return first, second


def body(wavefn, cell_mats, conn, proj, coupling, support, bounds, rotation):
    my_dom = lax.axis_index("dom")
    dom_count = lax.axis_size("dom")
    node_count, vec_cols = wavefn.shape
    cell_count, cell_nodes = conn.shape
    atom_count, supp_count, proj_count, _ = proj.shape
    entry_count = atom_count * supp_count
    slot_cap = 2
    slot_count = dom_count * slot_cap
    blocks = node_count // LO
    first_pairs, second_pairs = pairs(dom_count)
    even = my_dom % 2 == 0
    side = (my_dom % 2).astype(jnp.int32).reshape(1)

    def swap_pairs(first, second):
        return (
            lax.ppermute(first, "dom", first_pairs),
            lax.ppermute(second, "dom", second_pairs),
        )

    def exchange(to_next, to_previous):
        first, second = swap_pairs(
            jnp.where(even, to_next, to_previous), jnp.where(even, to_previous, to_next)
        )
        return jnp.where(even, second, first), jnp.where(even, first, second)

    all_entries = support.reshape(dom_count, entry_count)
    entry_source = all_entries // cell_count
    entry_cell = all_entries % cell_count
    entry_atom = jnp.arange(entry_count, dtype=jnp.int32) // supp_count

    def slots_of(dom):
        here = (entry_source == dom).astype(jnp.int32)
        rank = jnp.cumsum(here, axis=1) - 1
        hit = here[:, :, None] * (
            rank[:, :, None] == jnp.arange(slot_cap, dtype=jnp.int32)
        ).astype(jnp.int32)
        cell = jnp.sum(hit * entry_cell[:, :, None], axis=1)
        atom = jnp.sum(hit * entry_atom[None, :, None], axis=1)
        return cell, atom

    offsets = (-1, 0, 1)
    slots = [slots_of((my_dom + offset) % dom_count) for offset in offsets]
    own_entries = lax.dynamic_slice_in_dim(all_entries, my_dom, 1, 0)[0]
    own_source = own_entries // cell_count
    positions = jnp.arange(entry_count, dtype=jnp.int32)
    earlier = (own_source[:, None] == own_source[None, :]) & (
        positions[None, :] < positions[:, None]
    )
    own_slot = own_source * slot_cap + jnp.sum(earlier.astype(jnp.int32), axis=1)

    slot_ids = jnp.arange(slot_count, dtype=jnp.int32)
    place = (slot_ids[:, None] == own_slot[None, :]).astype(jnp.int32)
    entry_of = jnp.sum(place * (positions[None, :] + 1), axis=1) - 1
    outgoing = sort_out(entry_of, proj.reshape(entry_count, proj_count, cell_nodes), dom_count)
    outgoing, near_conn = lax.optimization_barrier((outgoing, conn))
    here = lax.all_to_all(outgoing, "dom", split_axis=0, concat_axis=0, tiled=True)
    conn_low, conn_high = exchange(near_conn, near_conn)
    own = wavefn.T

    conn_rows = conn.reshape(cell_count // STEP_CELLS, 1, STEP_CELLS * cell_nodes)
    mats = joined(cell_mats, 4, cell_count // STEP_CELLS)

    def local(state):
        image, *shared = local_part(side, state, conn_rows, mats)
        return image, swap_pairs(*shared)

    low, high = exchange(own[:, node_count - RIM :], own[:, :RIM])
    current = jnp.concatenate([low, own, high], axis=1)
    values = swap_pairs(here, here)
    node_rows, atom_rows = [], []
    for offset, cells, (cell, atom) in zip(offsets, (conn_low, conn, conn_high), slots):
        node = cells[cell] + offset * node_count
        node_rows.append(node)
        atom_rows.append(jnp.broadcast_to(atom[:, :, None], node.shape))
    node_row = jnp.stack(node_rows, axis=1).reshape(dom_count, 1, -1)
    atom_row = jnp.stack(atom_rows, axis=1).reshape(dom_count, 1, -1)
    inside = (node_row >= 0) & (node_row < node_count + 2 * RIM)
    high_part = jnp.where(inside, node_row // LO, -1)
    low_part = jnp.where(inside, node_row % LO, 0)
    coeffs = first_coeffs(here, atom_row, high_part, low_part, current)
    coeffs, values = lax.optimization_barrier((coeffs, values))
    values_low, values_high = (jnp.where(even, values[i], values[1 - i]) for i in (1, 0))

    pair = jnp.zeros((atom_count * proj_count,) * 2, F32)
    for a in range(atom_count):
        pair = lax.dynamic_update_slice(pair, coupling[a], (a * proj_count, a * proj_count))

    me = lax.axis_index("band")
    rotation_pieces = rotation.reshape(-1, vec_cols, vec_cols)
    swaps = [[(i, i ^ k) for i in range(4)] for k in range(4)]

    def rows_for(band):
        return lax.dynamic_index_in_dim(rotation_pieces, band, 0, keepdims=False)

    rotation_rows = [rows_for(me)]
    for k in range(1, 4):
        rotation_rows.append(lax.ppermute(rows_for(me ^ k), "band", swaps[k]))
    rotation_rows = jnp.stack(rotation_rows)

    def swap(block):
        return lax.all_to_all(block, "dom", split_axis=0, concat_axis=0, tiled=True)

    lower, cut, upper = (bounds[0], bounds[1], bounds[2])
    half_width = (upper - cut) / 2
    center = (upper + cut) / 2
    sigma_first = half_width / (lower - center)
    sigma_now = sigma_first

    previous = current
    scal = jnp.stack([sigma_first / half_width, center, jnp.zeros_like(center)])
    for turn_index in range(DEG):
        last = turn_index == DEG - 1
        arrived = swap(coeffs)
        if turn_index:
            current, previous = finish(*begun, *shared), current
        else:
            table = assemble(
                values_low, here, values_high, atom_row, high_part, low_part, current.shape[1]
            )
        coupled = couple(arrived, pair)
        coupled, current, table, mats = lax.optimization_barrier((coupled, current, table, mats))
        if turn_index == 1:
            coupled, rotation_rows = lax.optimization_barrier((coupled, rotation_rows))
        image, shared = local(current)
        weights = swap(coupled)
        args = (table, weights, current, previous, image)
        if last:
            done = settle(scal, side, final_turn(scal, *args), *shared)
        else:
            part, coeffs = begin(scal, *args)
            begun = (scal, side, *args, part)
            coeffs, shared = lax.optimization_barrier((coeffs, shared))
        sigma_next = 1 / (2 / sigma_first - sigma_now)
        scal = jnp.stack([2 * sigma_next / half_width, center, sigma_now * sigma_next])
        sigma_now = sigma_next

    beside = lax.ppermute(done, "band", swaps[1])
    across = lax.ppermute(done, "band", swaps[2])
    last = lax.ppermute(across, "band", swaps[1])
    return rotate((done, beside, across, last), rotation_rows)


def solution(mesh):
    in_specs = (
        P("dom", "band"),
        P("dom", None, None),
        P("dom", None),
        P("dom", None, None, None),
        P("dom", None, None),
        P(),
        P(),
        P(None, "band"),
    )
    out_specs = P("dom", "band")
    return jax.shard_map(body, mesh=mesh, in_specs=in_specs, out_specs=out_specs, check_vma=False)
```

```python
import functools

import jax
import jax.numpy as jnp
from jax import lax
from jax.experimental import pallas as pl
from jax.experimental.pallas import tpu as pltpu
from jax.sharding import PartitionSpec as P

RIM = 512
DEG = 5
PADDED = 40
LO = 256
STEP_CELLS = 32
MIB = 1024 * 1024

BF16 = jnp.bfloat16
F32 = jnp.float32


def params(mib, *semantics):
    return pltpu.CompilerParams(dimension_semantics=semantics, vmem_limit_bytes=mib * MIB)


def dot(a, b, a_dim, b_dim, **kw):
    return lax.dot_general(
        a, b, (((a_dim,), (b_dim,)), ((), ())), preferred_element_type=F32, **kw
    )


def joined_kernel(cells, out):
    order = cells.shape[1]
    out[...] = jnp.zeros_like(out)
    for group in range(out.shape[0]):
        for i in range(out.shape[1] // order):
            part = pl.ds(i * order, order)
            out[group, part, part] = cells[group * (out.shape[1] // order) + i]


def joined(cell_mats, join, steps):
    cell_count, order, _ = cell_mats.shape
    groups = cell_count // join // steps
    return pl.pallas_call(
        joined_kernel,
        grid=(steps,),
        in_specs=[pl.BlockSpec((groups * join, order, order), lambda s: (s, 0, 0))],
        out_specs=pl.BlockSpec((groups, join * order, join * order), lambda s: (s, 0, 0)),
        out_shape=jax.ShapeDtypeStruct(
            (cell_count // join, join * order, join * order), BF16
        ),
        compiler_params=params(12, "arbitrary"),
        name="joined",
    )(cell_mats)


def local_kernel(side, state, conn, mats, image, first, second, packed, total):
    step = pl.program_id(0)
    cols = state.shape[0]
    half = packed.shape[1]

    @pl.when(step == 0)
    def _():
        packed[:cols] = state[:, :half]
        packed[cols:] = state[:, half:]

    index = conn[0]
    entries = index.shape[1]
    upper = index >= half
    within = jnp.where(upper, index - half, index).astype(jnp.int16)
    row = lax.broadcasted_iota(jnp.int16, (half, entries), 0)
    hot = jnp.where(row == within, BF16(1.0), BF16(0.0))
    both = dot(packed[...], hot, 1, 0)
    vals = jnp.where(upper, both[cols:], both[:cols]).astype(BF16)
    width = mats.shape[1]
    term = jnp.concatenate(
        [
            dot(vals[:, i * width : (i + 1) * width], mats[i], 1, 1)
            for i in range(entries // width)
        ],
        axis=1,
    )
    spread = jnp.concatenate(
        [jnp.where(upper, 0.0, term), jnp.where(upper, term, 0.0)], axis=0
    ).astype(BF16)
    part = dot(spread, hot, 1, 1)

    @pl.when(step == 0)
    def _():
        total[...] = part

    @pl.when(step > 0)
    def _():
        total[...] += part

    @pl.when(step == pl.num_programs(0) - 1)
    def _():
        image[:, :half] = total[:cols]
        image[:, half:] = total[cols:]
        to_previous = total[:cols, : 2 * RIM].astype(BF16)
        to_next = total[cols:, half - 2 * RIM :].astype(BF16)
        even = side[0] == 0
        first[...] = jnp.where(even, to_next, to_previous)
        second[...] = jnp.where(even, to_previous, to_next)


def local_part(side, state, conn_rows, mats):
    cols, ext_count = state.shape
    steps, _, entries = conn_rows.shape
    half = ext_count // 2
    groups = mats.shape[0] // steps
    width = mats.shape[1]
    whole = lambda s: (0, 0)
    shared = jax.ShapeDtypeStruct((cols, 2 * RIM), BF16)
    return pl.pallas_call(
        local_kernel,
        grid=(steps,),
        in_specs=[
            pl.BlockSpec(memory_space=pltpu.SMEM),
            pl.BlockSpec((cols, ext_count), whole),
            pl.BlockSpec((1, 1, entries), lambda s: (s, 0, 0)),
            pl.BlockSpec((groups, width, width), lambda s: (s, 0, 0)),
        ],
        out_specs=[
            pl.BlockSpec((cols, ext_count), whole),
            pl.BlockSpec((cols, 2 * RIM), whole),
            pl.BlockSpec((cols, 2 * RIM), whole),
        ],
        out_shape=[jax.ShapeDtypeStruct((cols, ext_count), F32), shared, shared],
        scratch_shapes=[
            pltpu.VMEM((2 * cols, half), BF16),
            pltpu.VMEM((2 * cols, half), F32),
        ],
        compiler_params=params(56, "arbitrary"),
        cost_estimate=pl.CostEstimate(
            flops=2 * 2 * steps * entries * half * 2 * cols,
            bytes_accessed=6 * MIB,
            transcendentals=0,
        ),
        name="local_part",
    )(side, state, conn_rows, mats)


def sort_out_kernel(entry_of, proj, out):
    dom_count = out.shape[0]
    cap = entry_of.shape[0] // dom_count

    def one(slot):
        entry = entry_of[slot]
        share = jnp.where(entry >= 0, 1.0, 0.0)
        return proj[jnp.maximum(entry, 0)].astype(F32) * share

    @pl.loop(0, dom_count, unroll=8)
    def _(dom):
        out[dom] = jnp.concatenate(
            [one(dom * cap + j) for j in range(cap)], axis=1
        ).astype(BF16)


def sort_out(entry_of, proj, dom_count):
    entry_count, proj_count, cell_nodes = proj.shape
    cap = entry_of.shape[0] // dom_count
    return pl.pallas_call(
        sort_out_kernel,
        in_specs=[
            pl.BlockSpec(memory_space=pltpu.SMEM),
            pl.BlockSpec(memory_space=pltpu.VMEM),
        ],
        out_specs=pl.BlockSpec(memory_space=pltpu.VMEM),
        out_shape=jax.ShapeDtypeStruct((dom_count, proj_count, cap * cell_nodes), BF16),
        compiler_params=params(8),
        name="sort_out",
    )(entry_of, proj)


def at_nodes(values, atom, high, low, blocks):
    proj_count, entries = values.shape
    atoms = 2
    parts = [jnp.where(atom == a, values, 0.0) for a in range(atoms)]
    parts.append(jnp.zeros((PADDED - atoms * proj_count, entries), F32))
    rows = jnp.concatenate(parts, axis=0)
    spread = jnp.concatenate([jnp.where(high == h, rows, 0.0) for h in blocks], axis=0)
    row = lax.broadcasted_iota(jnp.int16, (LO, entries), 0)
    hot = jnp.where(row == low.astype(jnp.int16), BF16(1.0), BF16(0.0))
    return dot(spread.astype(BF16), hot, 1, 1)


def block_rows(pieces, at, rows):
    return jnp.concatenate(
        [piece[at * PADDED : at * PADDED + rows] for piece in pieces], axis=0
    ).astype(BF16)


def split_owners(stacked, out):
    owners, rows, _ = out.shape
    for i in range(owners):
        out[i] = stacked[i * rows : (i + 1) * rows].astype(BF16)


def stack_owners(weights, stacked):
    owners, rows, _ = weights.shape
    for i in range(owners):
        stacked[i * rows : (i + 1) * rows] = weights[i].astype(F32)


def first_kernel(here, atom, high, low, now, coeffs, table, stacked):
    owners = here.shape[0]
    rows = coeffs.shape[1]
    blocks = range(now.shape[1] // LO)
    pieces = [
        at_nodes(here[i].astype(F32), atom[i], high[i], low[i], blocks) for i in range(owners)
    ]
    for h in blocks:
        table[:, h * LO : (h + 1) * LO] = block_rows(pieces, h, rows)
    stacked[...] = dot(table[...], now[...], 1, 1)
    split_owners(stacked, coeffs)


def first_coeffs(here, atom_row, high_part, low_part, now):
    owner_count, proj_count, lanes = here.shape
    cols, ext_count = now.shape
    rows = 2 * proj_count
    group = 32
    index = pl.BlockSpec((group, 1, lanes), lambda s: (s, 0, 1))
    return pl.pallas_call(
        first_kernel,
        grid=(owner_count // group,),
        in_specs=[
            pl.BlockSpec((group, proj_count, lanes), lambda s: (s, 0, 0)),
            index,
            index,
            index,
            pl.BlockSpec((cols, ext_count), lambda s: (0, 0)),
        ],
        out_specs=pl.BlockSpec((group, rows, cols), lambda s: (s, 0, 0)),
        out_shape=jax.ShapeDtypeStruct((owner_count, rows, cols), BF16),
        scratch_shapes=[
            pltpu.VMEM((group * rows, ext_count), BF16),
            pltpu.VMEM((group * rows, cols), F32),
        ],
        compiler_params=params(48, "arbitrary"),
        cost_estimate=pl.CostEstimate(
            flops=2 * owner_count * rows * ext_count * (lanes + cols),
            bytes_accessed=2 * MIB,
            transcendentals=0,
        ),
        name="first_coeffs",
    )(here, atom_row, high_part, low_part, now)


def assemble_kernel(low, here, high, atom_row, high_part, low_part, out):
    owners, _, lanes = here.shape
    rows = out.shape[0] // owners
    block_count = out.shape[1] // LO
    edge = 2 * RIM // LO
    sides = (
        (low, here, slice(0, 2 * lanes), range(block_count - edge)),
        (here, high, slice(lanes, 3 * lanes), range(block_count - edge, block_count)),
    )
    for left, right, part, blocks in sides:
        pieces = []
        for i in range(owners):
            values = jnp.concatenate([left[i], right[i]], axis=1).astype(F32)
            pieces.append(
                at_nodes(
                    values, atom_row[i][:, part], high_part[i][:, part], low_part[i][:, part], blocks
                )
            )
        for at, h in enumerate(blocks):
            out[:, h * LO : (h + 1) * LO] = block_rows(pieces, at, rows)


def assemble(low, here, high, atom_row, high_part, low_part, ext_count):
    owner_count, proj_count, lanes = here.shape
    entries = atom_row.shape[2]
    rows = 2 * proj_count
    group = 8
    values = pl.BlockSpec((group, proj_count, lanes), lambda s: (s, 0, 0))
    index = pl.BlockSpec((group, 1, entries), lambda s: (s, 0, 0))
    return pl.pallas_call(
        assemble_kernel,
        grid=(owner_count // group,),
        in_specs=[values] * 3 + [index] * 3,
        out_specs=pl.BlockSpec((group * rows, ext_count), lambda s: (s, 0)),
        out_shape=jax.ShapeDtypeStruct((owner_count * rows, ext_count), BF16),
        compiler_params=params(56, "arbitrary"),
        cost_estimate=pl.CostEstimate(
            flops=2 * owner_count * rows * ext_count * entries,
            bytes_accessed=16 * MIB,
            transcendentals=0,
        ),
        name="assemble",
    )(low, here, high, atom_row, high_part, low_part)


def factors(bounds, turn_index):
    lower, cut, upper = (jnp.full((1, RIM), bounds[i], F32) for i in range(3))
    half_width = (upper - cut) / 2
    center = (upper + cut) / 2
    sigma_first = half_width / (lower - center)
    if turn_index == 0:
        return sigma_first / half_width, center, jnp.zeros_like(center)
    sigma_now = sigma_first
    for _ in range(turn_index - 1):
        sigma_now = 1 / (2 / sigma_first - sigma_now)
    sigma_next = 1 / (2 / sigma_first - sigma_now)
    return 2 * sigma_next / half_width, center, sigma_now * sigma_next


def begin_kernel(
    turn_index, bounds, table, weights, now, before, image, part, out, total, flipped
):
    step = pl.program_id(0)
    last = pl.num_programs(0) - 1
    edge = (step == 0) | (step == last)
    scal = factors(bounds, turn_index)

    def add(value):
        return dot(table[...], value.astype(BF16), 1, 1)

    @pl.when(step == 0)
    def _():
        stack_owners(weights, total)
        flipped[...] = total[...].T.astype(BF16)
        total[...] = add(scal[0] * image[...])

    @pl.when(jnp.logical_not(edge))
    def _():
        value = scal[0] * (
            image[...] + dot(flipped[...], table[...], 1, 0) - scal[1] * now[...].astype(F32)
        )
        value -= scal[2] * before[...].astype(F32)
        part[...] = value
        total[...] += add(value)

    @pl.when(step == last)
    def _():
        total[...] += add(scal[0] * image[...])
        split_owners(total, out)


def begin(turn_index, bounds, table, weights, now, before, image):
    rows, ext_count = table.shape
    cols = now.shape[0]
    steps = ext_count // RIM
    block = pl.BlockSpec((cols, RIM), lambda h: (0, h))
    inside = pl.BlockSpec((cols, RIM), lambda h: (0, jnp.clip(h - 1, 0, steps - 3)))
    whole = pl.BlockSpec(weights.shape, lambda h: (0, 0, 0))
    return pl.pallas_call(
        functools.partial(begin_kernel, turn_index),
        grid=(steps,),
        in_specs=[
            pl.BlockSpec(memory_space=pltpu.SMEM),
            pl.BlockSpec((rows, RIM), lambda h: (0, h)),
            whole,
            block,
            block,
            block,
        ],
        out_specs=[inside, whole],
        out_shape=[
            jax.ShapeDtypeStruct((cols, ext_count - 2 * RIM), F32),
            jax.ShapeDtypeStruct(weights.shape, BF16),
        ],
        scratch_shapes=[pltpu.VMEM((rows, cols), F32), pltpu.VMEM((cols, rows), BF16)],
        compiler_params=params(56, "arbitrary"),
        cost_estimate=pl.CostEstimate(
            flops=4 * rows * ext_count * cols,
            bytes_accessed=18 * MIB,
            transcendentals=0,
        ),
        name="begin",
    )(bounds, table, weights, now, before, image)


def finish_kernel(
    turn_index, bounds, side, table, weights, now, before, image, part, first, second,
    new, stacked, flipped,
):
    step = pl.program_id(0)
    last = pl.num_programs(0) - 1
    edge = (step == 0) | (step == last)
    scal = factors(bounds, turn_index)
    came = jnp.where((step <= 1) == (side[0] == 0), second[...], first[...]).astype(F32)
    came *= jnp.where((step <= 1) | (step >= last - 1), 1.0, 0.0)

    @pl.when(step == 0)
    def _():
        stack_owners(weights, stacked)
        flipped[...] = stacked[...].T.astype(BF16)

    @pl.when(edge)
    def _():
        value = image[...] + came + dot(flipped[...], table[...], 1, 0)
        value = scal[0] * (value - scal[1] * now[...].astype(F32))
        new[...] = (value - scal[2] * before[...].astype(F32)).astype(BF16)

    @pl.when(jnp.logical_not(edge))
    def _():
        new[...] = (part[...] + scal[0] * came).astype(BF16)


def finish(turn_index, bounds, side, table, weights, now, before, image, part, first, second):
    rows, ext_count = table.shape
    cols = now.shape[0]
    steps = ext_count // RIM
    block = pl.BlockSpec((cols, RIM), lambda h: (0, h))

    def ends(h):
        return (0, jnp.where(h < steps - 2, 0, steps - 1))

    def shared(h):
        return (0, jnp.where((h == 0) | (h == steps - 2), 0, 1))

    return pl.pallas_call(
        functools.partial(finish_kernel, turn_index),
        grid=(steps,),
        in_specs=[
            pl.BlockSpec(memory_space=pltpu.SMEM),
            pl.BlockSpec(memory_space=pltpu.SMEM),
            pl.BlockSpec((rows, RIM), ends),
            pl.BlockSpec(weights.shape, lambda h: (0, 0, 0)),
            pl.BlockSpec((cols, RIM), ends),
            pl.BlockSpec((cols, RIM), ends),
            pl.BlockSpec((cols, RIM), ends),
            pl.BlockSpec((cols, RIM), lambda h: (0, jnp.clip(h - 1, 0, steps - 3))),
            pl.BlockSpec((cols, RIM), shared),
            pl.BlockSpec((cols, RIM), shared),
        ],
        out_specs=block,
        out_shape=jax.ShapeDtypeStruct((cols, ext_count), BF16),
        scratch_shapes=[pltpu.VMEM((rows, cols), F32), pltpu.VMEM((cols, rows), BF16)],
        compiler_params=params(56, "arbitrary"),
        cost_estimate=pl.CostEstimate(
            flops=4 * rows * RIM * cols, bytes_accessed=10 * MIB, transcendentals=0
        ),
        name="finish",
    )(bounds, side, table, weights, now, before, image, part, first, second)


def final_kernel(
    turn_index, bounds, table, weights, now, before, image, part, stacked, flipped
):
    step = pl.program_id(0)
    scal = factors(bounds, turn_index)

    @pl.when(step == 0)
    def _():
        stack_owners(weights, stacked)
        flipped[...] = stacked[...].T.astype(BF16)

    value = image[...] + dot(flipped[...], table[...], 1, 0)
    value = scal[0] * (value - scal[1] * now[...].astype(F32))
    part[...] = value - scal[2] * before[...].astype(F32)


def final_turn(turn_index, bounds, table, weights, now, before, image):
    rows, ext_count = table.shape
    cols = now.shape[0]
    steps = ext_count // RIM - 2
    inside = pl.BlockSpec((cols, RIM), lambda h: (0, h + 1))
    return pl.pallas_call(
        functools.partial(final_kernel, turn_index),
        grid=(steps,),
        in_specs=[
            pl.BlockSpec(memory_space=pltpu.SMEM),
            pl.BlockSpec((rows, RIM), lambda h: (0, h + 1)),
            pl.BlockSpec(weights.shape, lambda h: (0, 0, 0)),
            inside,
            inside,
            inside,
        ],
        out_specs=pl.BlockSpec((cols, RIM), lambda h: (0, h)),
        out_shape=jax.ShapeDtypeStruct((cols, ext_count - 2 * RIM), F32),
        scratch_shapes=[pltpu.VMEM((rows, cols), F32), pltpu.VMEM((cols, rows), BF16)],
        compiler_params=params(56, "arbitrary"),
        cost_estimate=pl.CostEstimate(
            flops=2 * rows * ext_count * cols, bytes_accessed=11 * MIB, transcendentals=0
        ),
        name="final_turn",
    )(bounds, table, weights, now, before, image)


def settle_kernel(turn_index, bounds, side, part, first, second, new):
    scal = factors(bounds, turn_index)
    even = side[0] == 0
    from_previous = jnp.where(even, second[:, RIM:], first[:, RIM:]).astype(F32)
    from_next = jnp.where(even, first[:, :RIM], second[:, :RIM]).astype(F32)
    end = part.shape[1] - RIM
    new[:, :RIM] = (part[:, :RIM] + scal[0] * from_previous).astype(BF16)
    new[:, RIM:end] = part[:, RIM:end].astype(BF16)
    new[:, end:] = (part[:, end:] + scal[0] * from_next).astype(BF16)


def settle(turn_index, bounds, side, part, first, second):
    smem = pl.BlockSpec(memory_space=pltpu.SMEM)
    vmem = pl.BlockSpec(memory_space=pltpu.VMEM)
    return pl.pallas_call(
        functools.partial(settle_kernel, turn_index),
        in_specs=[smem, smem, vmem, vmem, vmem],
        out_specs=vmem,
        out_shape=jax.ShapeDtypeStruct(part.shape, BF16),
        compiler_params=params(8),
        name="settle",
    )(bounds, side, part, first, second)


def rotate_kernel(first, second, third, fourth, mats, out):
    total = dot(first[...], mats[0], 0, 1)
    for i, piece in enumerate((second, third, fourth)):
        total += dot(piece[...], mats[i + 1], 0, 1)
    out[...] = total.astype(BF16)


def rotate(pieces, mats):
    cols, node_count = pieces[0].shape
    step = RIM
    block = pl.BlockSpec((cols, step), lambda h: (0, h))
    return pl.pallas_call(
        rotate_kernel,
        grid=(node_count // step,),
        in_specs=[block] * 4 + [pl.BlockSpec(mats.shape, lambda h: (0, 0, 0))],
        out_specs=pl.BlockSpec((step, cols), lambda h: (h, 0)),
        out_shape=jax.ShapeDtypeStruct((node_count, cols), BF16),
        compiler_params=params(12, "arbitrary"),
        name="rotate",
    )(*pieces, mats)


def couple_kernel(parts, coupling, out):
    coeffs = jnp.sum(parts[...].astype(F32), axis=0)
    weights = dot(coupling[...], coeffs, 1, 0, precision=lax.Precision.HIGHEST)
    out[...] = jnp.broadcast_to(weights.astype(BF16)[None], out.shape)


def couple(parts, coupling):
    return pl.pallas_call(
        couple_kernel,
        out_shape=jax.ShapeDtypeStruct(parts.shape, BF16),
        compiler_params=params(10),
        name="couple",
    )(parts, coupling)


def pairs(count):
    first = [(i, i ^ 1) for i in range(count)]
    second = [(i, (i + 1 if i % 2 else i - 1) % count) for i in range(count)]
    return first, second


def body(wavefn, cell_mats, conn, proj, coupling, support, bounds, rotation):
    my_dom = lax.axis_index("dom")
    dom_count = lax.axis_size("dom")
    node_count, vec_cols = wavefn.shape
    cell_count, cell_nodes = conn.shape
    atom_count, supp_count, proj_count, _ = proj.shape
    entry_count = atom_count * supp_count
    slot_cap = 2
    slot_count = dom_count * slot_cap
    blocks = node_count // LO
    first_pairs, second_pairs = pairs(dom_count)
    even = my_dom % 2 == 0
    side = (my_dom % 2).astype(jnp.int32).reshape(1)

    def swap_pairs(first, second):
        return (
            lax.ppermute(first, "dom", first_pairs),
            lax.ppermute(second, "dom", second_pairs),
        )

    def exchange(to_next, to_previous):
        first, second = swap_pairs(
            jnp.where(even, to_next, to_previous), jnp.where(even, to_previous, to_next)
        )
        return jnp.where(even, second, first), jnp.where(even, first, second)

    all_entries = support.reshape(dom_count, entry_count)
    entry_source = all_entries // cell_count
    entry_cell = all_entries % cell_count
    entry_atom = jnp.arange(entry_count, dtype=jnp.int32) // supp_count

    def slots_of(dom):
        here = (entry_source == dom).astype(jnp.int32)
        rank = jnp.cumsum(here, axis=1) - 1
        hit = here[:, :, None] * (
            rank[:, :, None] == jnp.arange(slot_cap, dtype=jnp.int32)
        ).astype(jnp.int32)
        cell = jnp.sum(hit * entry_cell[:, :, None], axis=1)
        atom = jnp.sum(hit * entry_atom[None, :, None], axis=1)
        return cell, atom

    offsets = (-1, 0, 1)
    slots = [slots_of((my_dom + offset) % dom_count) for offset in offsets]
    own_entries = lax.dynamic_slice_in_dim(all_entries, my_dom, 1, 0)[0]
    own_source = own_entries // cell_count
    positions = jnp.arange(entry_count, dtype=jnp.int32)
    earlier = (own_source[:, None] == own_source[None, :]) & (
        positions[None, :] < positions[:, None]
    )
    own_slot = own_source * slot_cap + jnp.sum(earlier.astype(jnp.int32), axis=1)

    slot_ids = jnp.arange(slot_count, dtype=jnp.int32)
    place = (slot_ids[:, None] == own_slot[None, :]).astype(jnp.int32)
    entry_of = jnp.sum(place * (positions[None, :] + 1), axis=1) - 1
    outgoing = sort_out(entry_of, proj.reshape(entry_count, proj_count, cell_nodes), dom_count)
    outgoing, near_conn = lax.optimization_barrier((outgoing, conn))
    here = lax.all_to_all(outgoing, "dom", split_axis=0, concat_axis=0, tiled=True)
    conn_low, conn_high = exchange(near_conn, near_conn)
    own = wavefn.T

    conn_rows = conn.reshape(cell_count // STEP_CELLS, 1, STEP_CELLS * cell_nodes)
    mats = joined(cell_mats, 4, cell_count // STEP_CELLS)

    def local(state):
        image, *shared = local_part(side, state, conn_rows, mats)
        return image, swap_pairs(*shared)

    low, high = exchange(own[:, node_count - RIM :], own[:, :RIM])
    current = jnp.concatenate([low, own, high], axis=1)
    here, conn_rows = lax.optimization_barrier((here, conn_rows))
    values = swap_pairs(here, here)
    node_rows, atom_rows = [], []
    for offset, cells, (cell, atom) in zip(offsets, (conn_low, conn, conn_high), slots):
        node = cells[cell] + offset * node_count
        node_rows.append(node)
        atom_rows.append(jnp.broadcast_to(atom[:, :, None], node.shape))
    node_row = jnp.stack(node_rows, axis=1).reshape(dom_count, 1, -1)
    atom_row = jnp.stack(atom_rows, axis=1).reshape(dom_count, 1, -1)
    inside = (node_row >= 0) & (node_row < node_count + 2 * RIM)
    high_part = jnp.where(inside, node_row // LO, -1)
    low_part = jnp.where(inside, node_row % LO, 0)
    coeffs = first_coeffs(here, atom_row, high_part, low_part, current)
    coeffs, values = lax.optimization_barrier((coeffs, values))
    values_low, values_high = (jnp.where(even, values[i], values[1 - i]) for i in (1, 0))

    pair = jnp.zeros((atom_count * proj_count,) * 2, F32)
    for a in range(atom_count):
        pair = lax.dynamic_update_slice(pair, coupling[a], (a * proj_count, a * proj_count))

    me = lax.axis_index("band")
    rotation_pieces = rotation.reshape(-1, vec_cols, vec_cols)
    swaps = [[(i, i ^ k) for i in range(4)] for k in range(4)]

    def rows_for(band):
        return lax.dynamic_index_in_dim(rotation_pieces, band, 0, keepdims=False)

    rotation_rows = [rows_for(me)]
    for k in range(1, 4):
        rotation_rows.append(lax.ppermute(rows_for(me ^ k), "band", swaps[k]))
    rotation_rows = jnp.stack(rotation_rows)

    def swap(block):
        return lax.all_to_all(block, "dom", split_axis=0, concat_axis=0, tiled=True)

    previous = current
    for turn_index in range(DEG):
        last = turn_index == DEG - 1
        arrived = swap(coeffs)
        if turn_index:
            current, previous = finish(*begun, *shared), current
        else:
            table = assemble(
                values_low, here, values_high, atom_row, high_part, low_part, current.shape[1]
            )
        coupled = couple(arrived, pair)
        coupled, current, table, mats = lax.optimization_barrier((coupled, current, table, mats))
        if turn_index == 1:
            coupled, rotation_rows = lax.optimization_barrier((coupled, rotation_rows))
        image, shared = local(current)
        weights = swap(coupled)
        args = (table, weights, current, previous, image)
        if last:
            done = settle(
                turn_index, bounds, side, final_turn(turn_index, bounds, *args), *shared
            )
        else:
            part, coeffs = begin(turn_index, bounds, *args)
            begun = (turn_index, bounds, side, *args, part)
            coeffs, shared = lax.optimization_barrier((coeffs, shared))

    beside = lax.ppermute(done, "band", swaps[1])
    across = lax.ppermute(done, "band", swaps[2])
    last = lax.ppermute(across, "band", swaps[1])
    return rotate((done, beside, across, last), rotation_rows)


def solution(mesh):
    in_specs = (
        P("dom", "band"),
        P("dom", None, None),
        P("dom", None),
        P("dom", None, None, None),
        P("dom", None, None),
        P(),
        P(),
        P(None, "band"),
    )
    out_specs = P("dom", "band")
    return jax.shard_map(body, mesh=mesh, in_specs=in_specs, out_specs=out_specs, check_vma=False)
```

```python
import functools

import jax
import jax.numpy as jnp
from jax import lax
from jax.experimental import pallas as pl
from jax.experimental.pallas import tpu as pltpu
from jax.sharding import PartitionSpec as P

RIM = 512
DEG = 5
PADDED = 40
LO = 256
STEP_CELLS = 32
MIB = 1024 * 1024

BF16 = jnp.bfloat16
F32 = jnp.float32


def params(mib, *semantics):
    return pltpu.CompilerParams(dimension_semantics=semantics, vmem_limit_bytes=mib * MIB)


def dot(a, b, a_dim, b_dim, **kw):
    return lax.dot_general(
        a, b, (((a_dim,), (b_dim,)), ((), ())), preferred_element_type=F32, **kw
    )


def joined_kernel(cells, out):
    order = cells.shape[1]
    out[...] = jnp.zeros_like(out)
    for group in range(out.shape[0]):
        for i in range(out.shape[1] // order):
            part = pl.ds(i * order, order)
            out[group, part, part] = cells[group * (out.shape[1] // order) + i]


def joined(cell_mats, join, steps):
    cell_count, order, _ = cell_mats.shape
    groups = cell_count // join // steps
    return pl.pallas_call(
        joined_kernel,
        grid=(steps,),
        in_specs=[pl.BlockSpec((groups * join, order, order), lambda s: (s, 0, 0))],
        out_specs=pl.BlockSpec((groups, join * order, join * order), lambda s: (s, 0, 0)),
        out_shape=jax.ShapeDtypeStruct(
            (cell_count // join, join * order, join * order), BF16
        ),
        compiler_params=params(12, "arbitrary"),
        name="joined",
    )(cell_mats)


def local_kernel(side, state, conn, mats, image, first, second, packed, total):
    step = pl.program_id(0)
    cols = state.shape[0]
    half = packed.shape[1]

    @pl.when(step == 0)
    def _():
        packed[:cols] = state[:, :half]
        packed[cols:] = state[:, half:]

    index = conn[0]
    entries = index.shape[1]
    upper = index >= half
    within = jnp.where(upper, index - half, index).astype(jnp.int16)
    row = lax.broadcasted_iota(jnp.int16, (half, entries), 0)
    hot = jnp.where(row == within, BF16(1.0), BF16(0.0))
    both = dot(packed[...], hot, 1, 0)
    vals = jnp.where(upper, both[cols:], both[:cols]).astype(BF16)
    width = mats.shape[1]
    term = jnp.concatenate(
        [
            dot(vals[:, i * width : (i + 1) * width], mats[i], 1, 1)
            for i in range(entries // width)
        ],
        axis=1,
    )
    spread = jnp.concatenate(
        [jnp.where(upper, 0.0, term), jnp.where(upper, term, 0.0)], axis=0
    ).astype(BF16)
    part = dot(spread, hot, 1, 1)

    @pl.when(step == 0)
    def _():
        total[...] = part

    @pl.when(step > 0)
    def _():
        total[...] += part

    @pl.when(step == pl.num_programs(0) - 1)
    def _():
        image[:, :half] = total[:cols]
        image[:, half:] = total[cols:]
        to_previous = total[:cols, : 2 * RIM].astype(BF16)
        to_next = total[cols:, half - 2 * RIM :].astype(BF16)
        even = side[0] == 0
        first[...] = jnp.where(even, to_next, to_previous)
        second[...] = jnp.where(even, to_previous, to_next)


def local_part(side, state, conn_rows, mats):
    cols, ext_count = state.shape
    steps, _, entries = conn_rows.shape
    half = ext_count // 2
    groups = mats.shape[0] // steps
    width = mats.shape[1]
    whole = lambda s: (0, 0)
    shared = jax.ShapeDtypeStruct((cols, 2 * RIM), BF16)
    return pl.pallas_call(
        local_kernel,
        grid=(steps,),
        in_specs=[
            pl.BlockSpec(memory_space=pltpu.SMEM),
            pl.BlockSpec((cols, ext_count), whole),
            pl.BlockSpec((1, 1, entries), lambda s: (s, 0, 0)),
            pl.BlockSpec((groups, width, width), lambda s: (s, 0, 0)),
        ],
        out_specs=[
            pl.BlockSpec((cols, ext_count), whole),
            pl.BlockSpec((cols, 2 * RIM), whole),
            pl.BlockSpec((cols, 2 * RIM), whole),
        ],
        out_shape=[jax.ShapeDtypeStruct((cols, ext_count), F32), shared, shared],
        scratch_shapes=[
            pltpu.VMEM((2 * cols, half), BF16),
            pltpu.VMEM((2 * cols, half), F32),
        ],
        compiler_params=params(56, "arbitrary"),
        cost_estimate=pl.CostEstimate(
            flops=2 * 2 * steps * entries * half * 2 * cols,
            bytes_accessed=6 * MIB,
            transcendentals=0,
        ),
        name="local_part",
    )(side, state, conn_rows, mats)


def sort_out_kernel(entry_of, proj, out):
    dom_count = out.shape[0]
    cap = entry_of.shape[0] // dom_count

    def one(slot):
        entry = entry_of[slot]
        share = jnp.where(entry >= 0, 1.0, 0.0)
        return proj[jnp.maximum(entry, 0)].astype(F32) * share

    @pl.loop(0, dom_count, unroll=8)
    def _(dom):
        out[dom] = jnp.concatenate(
            [one(dom * cap + j) for j in range(cap)], axis=1
        ).astype(BF16)


def sort_out(entry_of, proj, dom_count):
    entry_count, proj_count, cell_nodes = proj.shape
    cap = entry_of.shape[0] // dom_count
    return pl.pallas_call(
        sort_out_kernel,
        in_specs=[
            pl.BlockSpec(memory_space=pltpu.SMEM),
            pl.BlockSpec(memory_space=pltpu.VMEM),
        ],
        out_specs=pl.BlockSpec(memory_space=pltpu.VMEM),
        out_shape=jax.ShapeDtypeStruct((dom_count, proj_count, cap * cell_nodes), BF16),
        compiler_params=params(8),
        name="sort_out",
    )(entry_of, proj)


def at_nodes(values, atom, high, low, blocks):
    proj_count, entries = values.shape
    atoms = 2
    parts = [jnp.where(atom == a, values, 0.0) for a in range(atoms)]
    parts.append(jnp.zeros((PADDED - atoms * proj_count, entries), F32))
    rows = jnp.concatenate(parts, axis=0)
    spread = jnp.concatenate([jnp.where(high == h, rows, 0.0) for h in blocks], axis=0)
    row = lax.broadcasted_iota(jnp.int16, (LO, entries), 0)
    hot = jnp.where(row == low.astype(jnp.int16), BF16(1.0), BF16(0.0))
    return dot(spread.astype(BF16), hot, 1, 1)


def block_rows(pieces, at, rows):
    return jnp.concatenate(
        [piece[at * PADDED : at * PADDED + rows] for piece in pieces], axis=0
    ).astype(BF16)


def split_owners(stacked, out):
    owners, rows, _ = out.shape
    for i in range(owners):
        out[i] = stacked[i * rows : (i + 1) * rows].astype(BF16)


def stack_owners(weights, stacked):
    owners, rows, _ = weights.shape
    for i in range(owners):
        stacked[i * rows : (i + 1) * rows] = weights[i].astype(F32)


def first_kernel(here, atom, high, low, now, coeffs, table, stacked):
    owners = here.shape[0]
    rows = coeffs.shape[1]
    blocks = range(now.shape[1] // LO)
    pieces = [
        at_nodes(here[i].astype(F32), atom[i], high[i], low[i], blocks) for i in range(owners)
    ]
    for h in blocks:
        table[:, h * LO : (h + 1) * LO] = block_rows(pieces, h, rows)
    stacked[...] = dot(table[...], now[...], 1, 1)
    split_owners(stacked, coeffs)


def first_coeffs(here, atom_row, high_part, low_part, now):
    owner_count, proj_count, lanes = here.shape
    cols, ext_count = now.shape
    rows = 2 * proj_count
    group = 32
    index = pl.BlockSpec((group, 1, lanes), lambda s: (s, 0, 1))
    return pl.pallas_call(
        first_kernel,
        grid=(owner_count // group,),
        in_specs=[
            pl.BlockSpec((group, proj_count, lanes), lambda s: (s, 0, 0)),
            index,
            index,
            index,
            pl.BlockSpec((cols, ext_count), lambda s: (0, 0)),
        ],
        out_specs=pl.BlockSpec((group, rows, cols), lambda s: (s, 0, 0)),
        out_shape=jax.ShapeDtypeStruct((owner_count, rows, cols), BF16),
        scratch_shapes=[
            pltpu.VMEM((group * rows, ext_count), BF16),
            pltpu.VMEM((group * rows, cols), F32),
        ],
        compiler_params=params(48, "arbitrary"),
        cost_estimate=pl.CostEstimate(
            flops=2 * owner_count * rows * ext_count * (lanes + cols),
            bytes_accessed=2 * MIB,
            transcendentals=0,
        ),
        name="first_coeffs",
    )(here, atom_row, high_part, low_part, now)


def assemble_kernel(side, first, here, second, atom_row, high_part, low_part, out):
    owners, _, lanes = here.shape
    rows = out.shape[0] // owners
    block_count = out.shape[1] // LO
    even = side[0] == 0
    edge = 2 * RIM // LO
    sides = (
        (True, slice(0, 2 * lanes), range(block_count - edge)),
        (False, slice(lanes, 3 * lanes), range(block_count - edge, block_count)),
    )
    for from_low, part, blocks in sides:
        pieces = []
        for i in range(owners):
            other = jnp.where(even == from_low, second[i].astype(F32), first[i].astype(F32))
            own = here[i].astype(F32)
            values = jnp.concatenate([other, own] if from_low else [own, other], axis=1)
            pieces.append(
                at_nodes(
                    values, atom_row[i][:, part], high_part[i][:, part], low_part[i][:, part], blocks
                )
            )
        for at, h in enumerate(blocks):
            out[:, h * LO : (h + 1) * LO] = block_rows(pieces, at, rows)


def assemble(side, first, here, second, atom_row, high_part, low_part, ext_count):
    owner_count, proj_count, lanes = here.shape
    entries = atom_row.shape[2]
    rows = 2 * proj_count
    group = 8
    values = pl.BlockSpec((group, proj_count, lanes), lambda s: (s, 0, 0))
    index = pl.BlockSpec((group, 1, entries), lambda s: (s, 0, 0))
    return pl.pallas_call(
        assemble_kernel,
        grid=(owner_count // group,),
        in_specs=[pl.BlockSpec(memory_space=pltpu.SMEM)] + [values] * 3 + [index] * 3,
        out_specs=pl.BlockSpec((group * rows, ext_count), lambda s: (s, 0)),
        out_shape=jax.ShapeDtypeStruct((owner_count * rows, ext_count), BF16),
        compiler_params=params(56, "arbitrary"),
        cost_estimate=pl.CostEstimate(
            flops=2 * owner_count * rows * ext_count * entries,
            bytes_accessed=16 * MIB,
            transcendentals=0,
        ),
        name="assemble",
    )(side, first, here, second, atom_row, high_part, low_part)


def factors(bounds, turn_index):
    lower, cut, upper = (jnp.full((1, RIM), bounds[i], F32) for i in range(3))
    half_width = (upper - cut) / 2
    center = (upper + cut) / 2
    sigma_first = half_width / (lower - center)
    if turn_index == 0:
        return sigma_first / half_width, center, jnp.zeros_like(center)
    sigma_now = sigma_first
    for _ in range(turn_index - 1):
        sigma_now = 1 / (2 / sigma_first - sigma_now)
    sigma_next = 1 / (2 / sigma_first - sigma_now)
    return 2 * sigma_next / half_width, center, sigma_now * sigma_next


def begin_kernel(
    turn_index, bounds, table, weights, now, before, image, part, out, total, flipped
):
    step = pl.program_id(0)
    last = pl.num_programs(0) - 1
    edge = (step == 0) | (step == last)
    scal = factors(bounds, turn_index)

    def add(value):
        return dot(table[...], value.astype(BF16), 1, 1)

    @pl.when(step == 0)
    def _():
        stack_owners(weights, total)
        flipped[...] = total[...].T.astype(BF16)
        total[...] = add(scal[0] * image[...])

    @pl.when(jnp.logical_not(edge))
    def _():
        value = scal[0] * (
            image[...] + dot(flipped[...], table[...], 1, 0) - scal[1] * now[...].astype(F32)
        )
        value -= scal[2] * before[...].astype(F32)
        part[...] = value
        total[...] += add(value)

    @pl.when(step == last)
    def _():
        total[...] += add(scal[0] * image[...])
        split_owners(total, out)


def begin(turn_index, bounds, table, weights, now, before, image):
    rows, ext_count = table.shape
    cols = now.shape[0]
    steps = ext_count // RIM
    block = pl.BlockSpec((cols, RIM), lambda h: (0, h))
    inside = pl.BlockSpec((cols, RIM), lambda h: (0, jnp.clip(h - 1, 0, steps - 3)))
    whole = pl.BlockSpec(weights.shape, lambda h: (0, 0, 0))
    return pl.pallas_call(
        functools.partial(begin_kernel, turn_index),
        grid=(steps,),
        in_specs=[
            pl.BlockSpec(memory_space=pltpu.SMEM),
            pl.BlockSpec((rows, RIM), lambda h: (0, h)),
            whole,
            block,
            block,
            block,
        ],
        out_specs=[inside, whole],
        out_shape=[
            jax.ShapeDtypeStruct((cols, ext_count - 2 * RIM), F32),
            jax.ShapeDtypeStruct(weights.shape, BF16),
        ],
        scratch_shapes=[pltpu.VMEM((rows, cols), F32), pltpu.VMEM((cols, rows), BF16)],
        compiler_params=params(54, "arbitrary"),
        cost_estimate=pl.CostEstimate(
            flops=4 * rows * ext_count * cols,
            bytes_accessed=18 * MIB,
            transcendentals=0,
        ),
        name="begin",
    )(bounds, table, weights, now, before, image)


def finish_kernel(
    turn_index, bounds, side, table, weights, now, before, image, part, first, second,
    new, stacked, flipped,
):
    step = pl.program_id(0)
    last = pl.num_programs(0) - 1
    edge = (step == 0) | (step == last)
    scal = factors(bounds, turn_index)
    came = jnp.where((step <= 1) == (side[0] == 0), second[...], first[...]).astype(F32)
    came *= jnp.where((step <= 1) | (step >= last - 1), 1.0, 0.0)

    @pl.when(step == 0)
    def _():
        stack_owners(weights, stacked)
        flipped[...] = stacked[...].T.astype(BF16)

    @pl.when(edge)
    def _():
        value = image[...] + came + dot(flipped[...], table[...], 1, 0)
        value = scal[0] * (value - scal[1] * now[...].astype(F32))
        new[...] = (value - scal[2] * before[...].astype(F32)).astype(BF16)

    @pl.when(jnp.logical_not(edge))
    def _():
        new[...] = (part[...] + scal[0] * came).astype(BF16)


def finish(turn_index, bounds, side, table, weights, now, before, image, part, first, second):
    rows, ext_count = table.shape
    cols = now.shape[0]
    steps = ext_count // RIM
    block = pl.BlockSpec((cols, RIM), lambda h: (0, h))

    def ends(h):
        return (0, jnp.where(h < steps - 2, 0, steps - 1))

    def shared(h):
        return (0, jnp.where((h == 0) | (h == steps - 2), 0, 1))

    return pl.pallas_call(
        functools.partial(finish_kernel, turn_index),
        grid=(steps,),
        in_specs=[
            pl.BlockSpec(memory_space=pltpu.SMEM),
            pl.BlockSpec(memory_space=pltpu.SMEM),
            pl.BlockSpec((rows, RIM), ends),
            pl.BlockSpec(weights.shape, lambda h: (0, 0, 0)),
            pl.BlockSpec((cols, RIM), ends),
            pl.BlockSpec((cols, RIM), ends),
            pl.BlockSpec((cols, RIM), ends),
            pl.BlockSpec((cols, RIM), lambda h: (0, jnp.clip(h - 1, 0, steps - 3))),
            pl.BlockSpec((cols, RIM), shared),
            pl.BlockSpec((cols, RIM), shared),
        ],
        out_specs=block,
        out_shape=jax.ShapeDtypeStruct((cols, ext_count), BF16),
        scratch_shapes=[pltpu.VMEM((rows, cols), F32), pltpu.VMEM((cols, rows), BF16)],
        compiler_params=params(56, "arbitrary"),
        cost_estimate=pl.CostEstimate(
            flops=4 * rows * RIM * cols, bytes_accessed=10 * MIB, transcendentals=0
        ),
        name="finish",
    )(bounds, side, table, weights, now, before, image, part, first, second)


def final_kernel(
    turn_index, bounds, table, weights, now, before, image, part, stacked, flipped
):
    step = pl.program_id(0)
    scal = factors(bounds, turn_index)

    @pl.when(step == 0)
    def _():
        stack_owners(weights, stacked)
        flipped[...] = stacked[...].T.astype(BF16)

    value = image[...] + dot(flipped[...], table[...], 1, 0)
    value = scal[0] * (value - scal[1] * now[...].astype(F32))
    part[...] = value - scal[2] * before[...].astype(F32)


def final_turn(turn_index, bounds, table, weights, now, before, image):
    rows, ext_count = table.shape
    cols = now.shape[0]
    steps = ext_count // RIM - 2
    inside = pl.BlockSpec((cols, RIM), lambda h: (0, h + 1))
    return pl.pallas_call(
        functools.partial(final_kernel, turn_index),
        grid=(steps,),
        in_specs=[
            pl.BlockSpec(memory_space=pltpu.SMEM),
            pl.BlockSpec((rows, RIM), lambda h: (0, h + 1)),
            pl.BlockSpec(weights.shape, lambda h: (0, 0, 0)),
            inside,
            inside,
            inside,
        ],
        out_specs=pl.BlockSpec((cols, RIM), lambda h: (0, h)),
        out_shape=jax.ShapeDtypeStruct((cols, ext_count - 2 * RIM), F32),
        scratch_shapes=[pltpu.VMEM((rows, cols), F32), pltpu.VMEM((cols, rows), BF16)],
        compiler_params=params(54, "arbitrary"),
        cost_estimate=pl.CostEstimate(
            flops=2 * rows * ext_count * cols, bytes_accessed=11 * MIB, transcendentals=0
        ),
        name="final_turn",
    )(bounds, table, weights, now, before, image)


def settle_kernel(turn_index, bounds, side, part, first, second, new):
    scal = factors(bounds, turn_index)
    even = side[0] == 0
    from_previous = jnp.where(even, second[:, RIM:], first[:, RIM:]).astype(F32)
    from_next = jnp.where(even, first[:, :RIM], second[:, :RIM]).astype(F32)
    end = part.shape[1] - RIM
    new[:, :RIM] = (part[:, :RIM] + scal[0] * from_previous).astype(BF16)
    new[:, RIM:end] = part[:, RIM:end].astype(BF16)
    new[:, end:] = (part[:, end:] + scal[0] * from_next).astype(BF16)


def settle(turn_index, bounds, side, part, first, second):
    smem = pl.BlockSpec(memory_space=pltpu.SMEM)
    vmem = pl.BlockSpec(memory_space=pltpu.VMEM)
    return pl.pallas_call(
        functools.partial(settle_kernel, turn_index),
        in_specs=[smem, smem, vmem, vmem, vmem],
        out_specs=vmem,
        out_shape=jax.ShapeDtypeStruct(part.shape, BF16),
        compiler_params=params(8),
        name="settle",
    )(bounds, side, part, first, second)


def rotate_kernel(first, second, third, fourth, mats, out):
    total = dot(first[...], mats[0], 0, 1)
    for i, piece in enumerate((second, third, fourth)):
        total += dot(piece[...], mats[i + 1], 0, 1)
    out[...] = total.astype(BF16)


def rotate(pieces, mats):
    cols, node_count = pieces[0].shape
    step = RIM
    block = pl.BlockSpec((cols, step), lambda h: (0, h))
    return pl.pallas_call(
        rotate_kernel,
        grid=(node_count // step,),
        in_specs=[block] * 4 + [pl.BlockSpec(mats.shape, lambda h: (0, 0, 0))],
        out_specs=pl.BlockSpec((step, cols), lambda h: (h, 0)),
        out_shape=jax.ShapeDtypeStruct((node_count, cols), BF16),
        compiler_params=params(12, "arbitrary"),
        name="rotate",
    )(*pieces, mats)


def couple_kernel(parts, coupling, out):
    coeffs = jnp.sum(parts[...].astype(F32), axis=0)
    atoms, order, _ = coupling.shape
    weights = jnp.concatenate(
        [
            dot(
                coupling[a],
                coeffs[a * order : (a + 1) * order],
                1,
                0,
                precision=lax.Precision.HIGHEST,
            )
            for a in range(atoms)
        ],
        axis=0,
    )
    out[...] = jnp.broadcast_to(weights.astype(BF16)[None], out.shape)


def couple(parts, coupling):
    return pl.pallas_call(
        couple_kernel,
        out_shape=jax.ShapeDtypeStruct(parts.shape, BF16),
        compiler_params=params(10),
        name="couple",
    )(parts, coupling)


def pairs(count):
    first = [(i, i ^ 1) for i in range(count)]
    second = [(i, (i + 1 if i % 2 else i - 1) % count) for i in range(count)]
    return first, second


def body(wavefn, cell_mats, conn, proj, coupling, support, bounds, rotation):
    my_dom = lax.axis_index("dom")
    dom_count = lax.axis_size("dom")
    node_count, vec_cols = wavefn.shape
    cell_count, cell_nodes = conn.shape
    atom_count, supp_count, proj_count, _ = proj.shape
    entry_count = atom_count * supp_count
    slot_cap = 2
    slot_count = dom_count * slot_cap
    blocks = node_count // LO
    me = lax.axis_index("band")
    rotation_pieces = rotation.reshape(-1, vec_cols, vec_cols)
    swaps = [[(i, i ^ k) for i in range(4)] for k in range(4)]

    def rows_for(band):
        return lax.dynamic_index_in_dim(rotation_pieces, band, 0, keepdims=False)

    rotation_rows = [rows_for(me)]
    for k in range(1, 4):
        rotation_rows.append(lax.ppermute(rows_for(me ^ k), "band", swaps[k]))
    rotation_rows = jnp.stack(rotation_rows)

    first_pairs, second_pairs = pairs(dom_count)
    even = my_dom % 2 == 0
    side = (my_dom % 2).astype(jnp.int32).reshape(1)

    def swap_pairs(first, second):
        return (
            lax.ppermute(first, "dom", first_pairs),
            lax.ppermute(second, "dom", second_pairs),
        )

    def exchange(to_next, to_previous):
        first, second = swap_pairs(
            jnp.where(even, to_next, to_previous), jnp.where(even, to_previous, to_next)
        )
        return jnp.where(even, second, first), jnp.where(even, first, second)

    all_entries = support.reshape(dom_count, entry_count)
    entry_source = all_entries // cell_count
    entry_cell = all_entries % cell_count
    entry_atom = jnp.arange(entry_count, dtype=jnp.int32) // supp_count

    def slots_of(dom):
        here = (entry_source == dom).astype(jnp.int32)
        rank = jnp.cumsum(here, axis=1) - 1
        hit = here[:, :, None] * (
            rank[:, :, None] == jnp.arange(slot_cap, dtype=jnp.int32)
        ).astype(jnp.int32)
        cell = jnp.sum(hit * entry_cell[:, :, None], axis=1)
        atom = jnp.sum(hit * entry_atom[None, :, None], axis=1)
        return cell, atom

    offsets = (-1, 0, 1)
    slots = [slots_of((my_dom + offset) % dom_count) for offset in offsets]
    own_entries = lax.dynamic_slice_in_dim(all_entries, my_dom, 1, 0)[0]
    own_source = own_entries // cell_count
    positions = jnp.arange(entry_count, dtype=jnp.int32)
    earlier = (own_source[:, None] == own_source[None, :]) & (
        positions[None, :] < positions[:, None]
    )
    own_slot = own_source * slot_cap + jnp.sum(earlier.astype(jnp.int32), axis=1)

    slot_ids = jnp.arange(slot_count, dtype=jnp.int32)
    place = (slot_ids[:, None] == own_slot[None, :]).astype(jnp.int32)
    entry_of = jnp.sum(place * (positions[None, :] + 1), axis=1) - 1
    outgoing = sort_out(entry_of, proj.reshape(entry_count, proj_count, cell_nodes), dom_count)
    outgoing, near_conn = lax.optimization_barrier((outgoing, conn))
    here = lax.all_to_all(outgoing, "dom", split_axis=0, concat_axis=0, tiled=True)
    conn_low, conn_high = exchange(near_conn, near_conn)
    own = wavefn.T

    conn_rows = conn.reshape(cell_count // STEP_CELLS, 1, STEP_CELLS * cell_nodes)
    mats = joined(cell_mats, 4, cell_count // STEP_CELLS)

    def local(state):
        image, *shared = local_part(side, state, conn_rows, mats)
        return image, swap_pairs(*shared)

    low, high = exchange(own[:, node_count - RIM :], own[:, :RIM])
    current = jnp.concatenate([low, own, high], axis=1)
    here, conn_rows, rotation_rows = lax.optimization_barrier((here, conn_rows, rotation_rows))
    values = swap_pairs(here, here)
    node_rows, atom_rows = [], []
    for offset, cells, (cell, atom) in zip(offsets, (conn_low, conn, conn_high), slots):
        node = cells[cell] + offset * node_count
        node_rows.append(node)
        atom_rows.append(jnp.broadcast_to(atom[:, :, None], node.shape))
    node_row = jnp.stack(node_rows, axis=1).reshape(dom_count, 1, -1)
    atom_row = jnp.stack(atom_rows, axis=1).reshape(dom_count, 1, -1)
    inside = (node_row >= 0) & (node_row < node_count + 2 * RIM)
    high_part = jnp.where(inside, node_row // LO, -1)
    low_part = jnp.where(inside, node_row % LO, 0)
    coeffs = first_coeffs(here, atom_row, high_part, low_part, current)
    coeffs, values = lax.optimization_barrier((coeffs, values))

    def swap(block):
        return lax.all_to_all(block, "dom", split_axis=0, concat_axis=0, tiled=True)

    previous = current
    for turn_index in range(DEG):
        last = turn_index == DEG - 1
        arrived = swap(coeffs)
        if turn_index:
            current, previous = finish(*begun, *shared), current
        else:
            table = assemble(
                side, values[0], here, values[1], atom_row, high_part, low_part, current.shape[1]
            )
        coupled = couple(arrived, coupling)
        coupled, current, table, mats = lax.optimization_barrier((coupled, current, table, mats))
        image, shared = local(current)
        weights = swap(coupled)
        args = (table, weights, current, previous, image)
        if last:
            done = settle(
                turn_index, bounds, side, final_turn(turn_index, bounds, *args), *shared
            )
        else:
            part, coeffs = begin(turn_index, bounds, *args)
            begun = (turn_index, bounds, side, *args, part)
            coeffs, shared = lax.optimization_barrier((coeffs, shared))

    beside = lax.ppermute(done, "band", swaps[1])
    across = lax.ppermute(done, "band", swaps[2])
    last = lax.ppermute(across, "band", swaps[1])
    return rotate((done, beside, across, last), rotation_rows)


def solution(mesh):
    in_specs = (
        P("dom", "band"),
        P("dom", None, None),
        P("dom", None),
        P("dom", None, None, None),
        P("dom", None, None),
        P(),
        P(),
        P(None, "band"),
    )
    out_specs = P("dom", "band")
    return jax.shard_map(body, mesh=mesh, in_specs=in_specs, out_specs=out_specs, check_vma=False)
```

```python
import functools

import jax
import jax.numpy as jnp
from jax import lax
from jax.experimental import pallas as pl
from jax.experimental.pallas import tpu as pltpu
from jax.sharding import PartitionSpec as P

RIM = 512
DEG = 5
PADDED = 40
LO = 256
STEP_CELLS = 32
MIB = 1024 * 1024

BF16 = jnp.bfloat16
F32 = jnp.float32


def params(mib, *semantics):
    return pltpu.CompilerParams(dimension_semantics=semantics, vmem_limit_bytes=mib * MIB)


def dot(a, b, a_dim, b_dim, **kw):
    return lax.dot_general(
        a, b, (((a_dim,), (b_dim,)), ((), ())), preferred_element_type=F32, **kw
    )


def joined_kernel(cells, out):
    order = cells.shape[1]
    out[...] = jnp.zeros_like(out)
    for group in range(out.shape[0]):
        for i in range(out.shape[1] // order):
            part = pl.ds(i * order, order)
            out[group, part, part] = cells[group * (out.shape[1] // order) + i]


def joined(cell_mats, join, steps):
    cell_count, order, _ = cell_mats.shape
    groups = cell_count // join // steps
    return pl.pallas_call(
        joined_kernel,
        grid=(steps,),
        in_specs=[pl.BlockSpec((groups * join, order, order), lambda s: (s, 0, 0))],
        out_specs=pl.BlockSpec((groups, join * order, join * order), lambda s: (s, 0, 0)),
        out_shape=jax.ShapeDtypeStruct(
            (cell_count // join, join * order, join * order), BF16
        ),
        compiler_params=params(12, "arbitrary"),
        name="joined",
    )(cell_mats)


def local_kernel(side, state, conn, mats, image, first, second, packed, total):
    step = pl.program_id(0)
    cols = state.shape[0]
    half = packed.shape[1]

    @pl.when(step == 0)
    def _():
        packed[:cols] = state[:, :half]
        packed[cols:] = state[:, half:]

    index = conn[0]
    entries = index.shape[1]
    upper = index >= half
    within = jnp.where(upper, index - half, index).astype(jnp.int16)
    row = lax.broadcasted_iota(jnp.int16, (half, entries), 0)
    hot = jnp.where(row == within, BF16(1.0), BF16(0.0))
    both = dot(packed[...], hot, 1, 0)
    vals = jnp.where(upper, both[cols:], both[:cols]).astype(BF16)
    width = mats.shape[1]
    term = jnp.concatenate(
        [
            dot(vals[:, i * width : (i + 1) * width], mats[i], 1, 1)
            for i in range(entries // width)
        ],
        axis=1,
    )
    spread = jnp.concatenate(
        [jnp.where(upper, 0.0, term), jnp.where(upper, term, 0.0)], axis=0
    ).astype(BF16)
    part = dot(spread, hot, 1, 1)

    @pl.when(step == 0)
    def _():
        total[...] = part

    @pl.when(step > 0)
    def _():
        total[...] += part

    @pl.when(step == pl.num_programs(0) - 1)
    def _():
        image[:, :half] = total[:cols]
        image[:, half:] = total[cols:]
        to_previous = total[:cols, : 2 * RIM].astype(BF16)
        to_next = total[cols:, half - 2 * RIM :].astype(BF16)
        even = side[0] == 0
        first[...] = jnp.where(even, to_next, to_previous)
        second[...] = jnp.where(even, to_previous, to_next)


def local_part(side, state, conn_rows, mats):
    cols, ext_count = state.shape
    steps, _, entries = conn_rows.shape
    half = ext_count // 2
    groups = mats.shape[0] // steps
    width = mats.shape[1]
    whole = lambda s: (0, 0)
    shared = jax.ShapeDtypeStruct((cols, 2 * RIM), BF16)
    return pl.pallas_call(
        local_kernel,
        grid=(steps,),
        in_specs=[
            pl.BlockSpec(memory_space=pltpu.SMEM),
            pl.BlockSpec((cols, ext_count), whole),
            pl.BlockSpec((1, 1, entries), lambda s: (s, 0, 0)),
            pl.BlockSpec((groups, width, width), lambda s: (s, 0, 0)),
        ],
        out_specs=[
            pl.BlockSpec((cols, ext_count), whole),
            pl.BlockSpec((cols, 2 * RIM), whole),
            pl.BlockSpec((cols, 2 * RIM), whole),
        ],
        out_shape=[jax.ShapeDtypeStruct((cols, ext_count), F32), shared, shared],
        scratch_shapes=[
            pltpu.VMEM((2 * cols, half), BF16),
            pltpu.VMEM((2 * cols, half), F32),
        ],
        compiler_params=params(56, "arbitrary"),
        cost_estimate=pl.CostEstimate(
            flops=2 * 2 * steps * entries * half * 2 * cols,
            bytes_accessed=6 * MIB,
            transcendentals=0,
        ),
        name="local_part",
    )(side, state, conn_rows, mats)


def sort_out_kernel(entry_of, proj, out):
    dom_count = out.shape[0]
    cap = entry_of.shape[0] // dom_count

    def one(slot):
        entry = entry_of[slot]
        share = jnp.where(entry >= 0, 1.0, 0.0)
        return proj[jnp.maximum(entry, 0)].astype(F32) * share

    @pl.loop(0, dom_count, unroll=8)
    def _(dom):
        out[dom] = jnp.concatenate(
            [one(dom * cap + j) for j in range(cap)], axis=1
        ).astype(BF16)


def sort_out(entry_of, proj, dom_count):
    entry_count, proj_count, cell_nodes = proj.shape
    cap = entry_of.shape[0] // dom_count
    return pl.pallas_call(
        sort_out_kernel,
        in_specs=[
            pl.BlockSpec(memory_space=pltpu.SMEM),
            pl.BlockSpec(memory_space=pltpu.VMEM),
        ],
        out_specs=pl.BlockSpec(memory_space=pltpu.VMEM),
        out_shape=jax.ShapeDtypeStruct((dom_count, proj_count, cap * cell_nodes), BF16),
        compiler_params=params(8),
        name="sort_out",
    )(entry_of, proj)


def at_nodes(values, atom, high, low, blocks):
    proj_count, entries = values.shape
    atoms = 2
    parts = [jnp.where(atom == a, values, 0.0) for a in range(atoms)]
    parts.append(jnp.zeros((PADDED - atoms * proj_count, entries), F32))
    rows = jnp.concatenate(parts, axis=0)
    spread = jnp.concatenate([jnp.where(high == h, rows, 0.0) for h in blocks], axis=0)
    row = lax.broadcasted_iota(jnp.int16, (LO, entries), 0)
    hot = jnp.where(row == low.astype(jnp.int16), BF16(1.0), BF16(0.0))
    return dot(spread.astype(BF16), hot, 1, 1)


def block_rows(pieces, at, rows):
    return jnp.concatenate(
        [piece[at * PADDED : at * PADDED + rows] for piece in pieces], axis=0
    ).astype(BF16)


def split_owners(stacked, out):
    owners, rows, _ = out.shape
    for i in range(owners):
        out[i] = stacked[i * rows : (i + 1) * rows].astype(BF16)


def stack_owners(weights, stacked):
    owners, rows, _ = weights.shape
    for i in range(owners):
        stacked[i * rows : (i + 1) * rows] = weights[i].astype(F32)


def first_kernel(here, atom, high, low, now, coeffs, table, stacked):
    owners = here.shape[0]
    rows = coeffs.shape[1]
    blocks = range(now.shape[1] // LO)
    pieces = [
        at_nodes(here[i].astype(F32), atom[i], high[i], low[i], blocks) for i in range(owners)
    ]
    for h in blocks:
        table[:, h * LO : (h + 1) * LO] = block_rows(pieces, h, rows)
    stacked[...] = dot(table[...], now[...], 1, 1)
    split_owners(stacked, coeffs)


def first_coeffs(here, atom_row, high_part, low_part, now):
    owner_count, proj_count, lanes = here.shape
    cols, ext_count = now.shape
    rows = 2 * proj_count
    group = 32
    index = pl.BlockSpec((group, 1, lanes), lambda s: (s, 0, 1))
    return pl.pallas_call(
        first_kernel,
        grid=(owner_count // group,),
        in_specs=[
            pl.BlockSpec((group, proj_count, lanes), lambda s: (s, 0, 0)),
            index,
            index,
            index,
            pl.BlockSpec((cols, ext_count), lambda s: (0, 0)),
        ],
        out_specs=pl.BlockSpec((group, rows, cols), lambda s: (s, 0, 0)),
        out_shape=jax.ShapeDtypeStruct((owner_count, rows, cols), BF16),
        scratch_shapes=[
            pltpu.VMEM((group * rows, ext_count), BF16),
            pltpu.VMEM((group * rows, cols), F32),
        ],
        compiler_params=params(48, "arbitrary"),
        cost_estimate=pl.CostEstimate(
            flops=2 * owner_count * rows * ext_count * (lanes + cols),
            bytes_accessed=2 * MIB,
            transcendentals=0,
        ),
        name="first_coeffs",
    )(here, atom_row, high_part, low_part, now)


def assemble_kernel(side, first, here, second, atom_row, high_part, low_part, out):
    owners, _, lanes = here.shape
    rows = out.shape[0] // owners
    block_count = out.shape[1] // LO
    even = side[0] == 0
    edge = 2 * RIM // LO
    sides = (
        (True, slice(0, 2 * lanes), range(block_count - edge)),
        (False, slice(lanes, 3 * lanes), range(block_count - edge, block_count)),
    )
    for from_low, part, blocks in sides:
        pieces = []
        for i in range(owners):
            other = jnp.where(even == from_low, second[i].astype(F32), first[i].astype(F32))
            own = here[i].astype(F32)
            values = jnp.concatenate([other, own] if from_low else [own, other], axis=1)
            pieces.append(
                at_nodes(
                    values, atom_row[i][:, part], high_part[i][:, part], low_part[i][:, part], blocks
                )
            )
        for at, h in enumerate(blocks):
            out[:, h * LO : (h + 1) * LO] = block_rows(pieces, at, rows)


def assemble(side, first, here, second, atom_row, high_part, low_part, ext_count):
    owner_count, proj_count, lanes = here.shape
    entries = atom_row.shape[2]
    rows = 2 * proj_count
    group = 8
    values = pl.BlockSpec((group, proj_count, lanes), lambda s: (s, 0, 0))
    index = pl.BlockSpec((group, 1, entries), lambda s: (s, 0, 0))
    return pl.pallas_call(
        assemble_kernel,
        grid=(owner_count // group,),
        in_specs=[pl.BlockSpec(memory_space=pltpu.SMEM)] + [values] * 3 + [index] * 3,
        out_specs=pl.BlockSpec((group * rows, ext_count), lambda s: (s, 0)),
        out_shape=jax.ShapeDtypeStruct((owner_count * rows, ext_count), BF16),
        compiler_params=params(56, "arbitrary"),
        cost_estimate=pl.CostEstimate(
            flops=2 * owner_count * rows * ext_count * entries,
            bytes_accessed=16 * MIB,
            transcendentals=0,
        ),
        name="assemble",
    )(side, first, here, second, atom_row, high_part, low_part)


def factors(bounds, turn_index):
    lower, cut, upper = (jnp.full((1, RIM), bounds[i], F32) for i in range(3))
    half_width = (upper - cut) / 2
    center = (upper + cut) / 2
    sigma_first = half_width / (lower - center)
    if turn_index == 0:
        return sigma_first / half_width, center, jnp.zeros_like(center)
    sigma_now = sigma_first
    for _ in range(turn_index - 1):
        sigma_now = 1 / (2 / sigma_first - sigma_now)
    sigma_next = 1 / (2 / sigma_first - sigma_now)
    return 2 * sigma_next / half_width, center, sigma_now * sigma_next


def begin_kernel(
    turn_index, bounds, table, weights, now, before, image, part, out, total, flipped
):
    step = pl.program_id(0)
    last = pl.num_programs(0) - 1
    edge = (step == 0) | (step == last)
    scal = factors(bounds, turn_index)

    def add(value):
        return dot(table[...], value.astype(BF16), 1, 1)

    @pl.when(step == 0)
    def _():
        stack_owners(weights, total)
        flipped[...] = total[...].T.astype(BF16)
        total[...] = add(scal[0] * image[...])

    @pl.when(jnp.logical_not(edge))
    def _():
        value = scal[0] * (
            image[...] + dot(flipped[...], table[...], 1, 0) - scal[1] * now[...].astype(F32)
        )
        value -= scal[2] * before[...].astype(F32)
        part[...] = value
        total[...] += add(value)

    @pl.when(step == last)
    def _():
        total[...] += add(scal[0] * image[...])
        split_owners(total, out)


def begin(turn_index, bounds, table, weights, now, before, image):
    rows, ext_count = table.shape
    cols = now.shape[0]
    steps = ext_count // RIM
    block = pl.BlockSpec((cols, RIM), lambda h: (0, h))
    inside = pl.BlockSpec((cols, RIM), lambda h: (0, jnp.clip(h - 1, 0, steps - 3)))
    whole = pl.BlockSpec(weights.shape, lambda h: (0, 0, 0))
    return pl.pallas_call(
        functools.partial(begin_kernel, turn_index),
        grid=(steps,),
        in_specs=[
            pl.BlockSpec(memory_space=pltpu.SMEM),
            pl.BlockSpec((rows, RIM), lambda h: (0, h)),
            whole,
            block,
            block,
            block,
        ],
        out_specs=[inside, whole],
        out_shape=[
            jax.ShapeDtypeStruct((cols, ext_count - 2 * RIM), F32),
            jax.ShapeDtypeStruct(weights.shape, BF16),
        ],
        scratch_shapes=[pltpu.VMEM((rows, cols), F32), pltpu.VMEM((cols, rows), BF16)],
        compiler_params=params(54, "arbitrary"),
        cost_estimate=pl.CostEstimate(
            flops=4 * rows * ext_count * cols,
            bytes_accessed=18 * MIB,
            transcendentals=0,
        ),
        name="begin",
    )(bounds, table, weights, now, before, image)


def finish_kernel(
    turn_index, bounds, side, table, weights, now, before, image, part, first, second,
    new, stacked, flipped,
):
    step = pl.program_id(0)
    last = pl.num_programs(0) - 1
    edge = (step == 0) | (step == last)
    scal = factors(bounds, turn_index)
    came = jnp.where((step <= 1) == (side[0] == 0), second[...], first[...]).astype(F32)
    came *= jnp.where((step <= 1) | (step >= last - 1), 1.0, 0.0)

    @pl.when(step == 0)
    def _():
        stack_owners(weights, stacked)
        flipped[...] = stacked[...].T.astype(BF16)

    @pl.when(edge)
    def _():
        value = image[...] + came + dot(flipped[...], table[...], 1, 0)
        value = scal[0] * (value - scal[1] * now[...].astype(F32))
        new[...] = (value - scal[2] * before[...].astype(F32)).astype(BF16)

    @pl.when(jnp.logical_not(edge))
    def _():
        new[...] = (part[...] + scal[0] * came).astype(BF16)


def finish(turn_index, bounds, side, table, weights, now, before, image, part, first, second):
    rows, ext_count = table.shape
    cols = now.shape[0]
    steps = ext_count // RIM
    block = pl.BlockSpec((cols, RIM), lambda h: (0, h))

    def ends(h):
        return (0, jnp.where(h < steps - 2, 0, steps - 1))

    def shared(h):
        return (0, jnp.where((h == 0) | (h == steps - 2), 0, 1))

    return pl.pallas_call(
        functools.partial(finish_kernel, turn_index),
        grid=(steps,),
        in_specs=[
            pl.BlockSpec(memory_space=pltpu.SMEM),
            pl.BlockSpec(memory_space=pltpu.SMEM),
            pl.BlockSpec((rows, RIM), ends),
            pl.BlockSpec(weights.shape, lambda h: (0, 0, 0)),
            pl.BlockSpec((cols, RIM), ends),
            pl.BlockSpec((cols, RIM), ends),
            pl.BlockSpec((cols, RIM), ends),
            pl.BlockSpec((cols, RIM), lambda h: (0, jnp.clip(h - 1, 0, steps - 3))),
            pl.BlockSpec((cols, RIM), shared),
            pl.BlockSpec((cols, RIM), shared),
        ],
        out_specs=block,
        out_shape=jax.ShapeDtypeStruct((cols, ext_count), BF16),
        scratch_shapes=[pltpu.VMEM((rows, cols), F32), pltpu.VMEM((cols, rows), BF16)],
        compiler_params=params(56, "arbitrary"),
        cost_estimate=pl.CostEstimate(
            flops=4 * rows * RIM * cols, bytes_accessed=10 * MIB, transcendentals=0
        ),
        name="finish",
    )(bounds, side, table, weights, now, before, image, part, first, second)


def final_kernel(
    turn_index, bounds, table, weights, now, before, image, part, stacked, flipped
):
    step = pl.program_id(0)
    scal = factors(bounds, turn_index)

    @pl.when(step == 0)
    def _():
        stack_owners(weights, stacked)
        flipped[...] = stacked[...].T.astype(BF16)

    value = image[...] + dot(flipped[...], table[...], 1, 0)
    value = scal[0] * (value - scal[1] * now[...].astype(F32))
    part[...] = value - scal[2] * before[...].astype(F32)


def final_turn(turn_index, bounds, table, weights, now, before, image):
    rows, ext_count = table.shape
    cols = now.shape[0]
    steps = ext_count // RIM - 2
    inside = pl.BlockSpec((cols, RIM), lambda h: (0, h + 1))
    return pl.pallas_call(
        functools.partial(final_kernel, turn_index),
        grid=(steps,),
        in_specs=[
            pl.BlockSpec(memory_space=pltpu.SMEM),
            pl.BlockSpec((rows, RIM), lambda h: (0, h + 1)),
            pl.BlockSpec(weights.shape, lambda h: (0, 0, 0)),
            inside,
            inside,
            inside,
        ],
        out_specs=pl.BlockSpec((cols, RIM), lambda h: (0, h)),
        out_shape=jax.ShapeDtypeStruct((cols, ext_count - 2 * RIM), F32),
        scratch_shapes=[pltpu.VMEM((rows, cols), F32), pltpu.VMEM((cols, rows), BF16)],
        compiler_params=params(54, "arbitrary"),
        cost_estimate=pl.CostEstimate(
            flops=2 * rows * ext_count * cols, bytes_accessed=11 * MIB, transcendentals=0
        ),
        name="final_turn",
    )(bounds, table, weights, now, before, image)


def settle_kernel(turn_index, bounds, side, part, first, second, new):
    scal = factors(bounds, turn_index)
    even = side[0] == 0
    from_previous = jnp.where(even, second[:, RIM:], first[:, RIM:]).astype(F32)
    from_next = jnp.where(even, first[:, :RIM], second[:, :RIM]).astype(F32)
    end = part.shape[1] - RIM
    new[:, :RIM] = (part[:, :RIM] + scal[0] * from_previous).astype(BF16)
    new[:, RIM:end] = part[:, RIM:end].astype(BF16)
    new[:, end:] = (part[:, end:] + scal[0] * from_next).astype(BF16)


def settle(turn_index, bounds, side, part, first, second):
    smem = pl.BlockSpec(memory_space=pltpu.SMEM)
    vmem = pl.BlockSpec(memory_space=pltpu.VMEM)
    return pl.pallas_call(
        functools.partial(settle_kernel, turn_index),
        in_specs=[smem, smem, vmem, vmem, vmem],
        out_specs=vmem,
        out_shape=jax.ShapeDtypeStruct(part.shape, BF16),
        compiler_params=params(56),
        name="settle",
    )(bounds, side, part, first, second)


def rotate_kernel(first, second, third, fourth, mats, out):
    total = dot(first[...], mats[0], 0, 1)
    for i, piece in enumerate((second, third, fourth)):
        total += dot(piece[...], mats[i + 1], 0, 1)
    out[...] = total.astype(BF16)


def rotate(pieces, mats):
    cols, node_count = pieces[0].shape
    step = RIM
    block = pl.BlockSpec((cols, step), lambda h: (0, h))
    return pl.pallas_call(
        rotate_kernel,
        grid=(node_count // step,),
        in_specs=[block] * 4 + [pl.BlockSpec(mats.shape, lambda h: (0, 0, 0))],
        out_specs=pl.BlockSpec((step, cols), lambda h: (h, 0)),
        out_shape=jax.ShapeDtypeStruct((node_count, cols), BF16),
        compiler_params=params(12, "arbitrary"),
        name="rotate",
    )(*pieces, mats)


def couple_kernel(parts, coupling, out):
    coeffs = jnp.sum(parts[...].astype(F32), axis=0)
    atoms, order, _ = coupling.shape
    weights = jnp.concatenate(
        [
            dot(
                coupling[a],
                coeffs[a * order : (a + 1) * order],
                1,
                0,
                precision=lax.Precision.HIGHEST,
            )
            for a in range(atoms)
        ],
        axis=0,
    )
    out[...] = jnp.broadcast_to(weights.astype(BF16)[None], out.shape)


def couple(parts, coupling):
    return pl.pallas_call(
        couple_kernel,
        out_shape=jax.ShapeDtypeStruct(parts.shape, BF16),
        compiler_params=params(10),
        name="couple",
    )(parts, coupling)


def pairs(count):
    first = [(i, i ^ 1) for i in range(count)]
    second = [(i, (i + 1 if i % 2 else i - 1) % count) for i in range(count)]
    return first, second


def body(wavefn, cell_mats, conn, proj, coupling, support, bounds, rotation):
    my_dom = lax.axis_index("dom")
    dom_count = lax.axis_size("dom")
    node_count, vec_cols = wavefn.shape
    cell_count, cell_nodes = conn.shape
    atom_count, supp_count, proj_count, _ = proj.shape
    entry_count = atom_count * supp_count
    slot_cap = 2
    slot_count = dom_count * slot_cap
    blocks = node_count // LO
    me = lax.axis_index("band")
    rotation_pieces = rotation.reshape(-1, vec_cols, vec_cols)
    swaps = [[(i, i ^ k) for i in range(4)] for k in range(4)]

    def rows_for(band):
        return lax.dynamic_index_in_dim(rotation_pieces, band, 0, keepdims=False)

    rotation_rows = [rows_for(me)]
    for k in range(1, 4):
        rotation_rows.append(lax.ppermute(rows_for(me ^ k), "band", swaps[k]))
    rotation_rows = jnp.stack(rotation_rows)

    first_pairs, second_pairs = pairs(dom_count)
    even = my_dom % 2 == 0
    side = (my_dom % 2).astype(jnp.int32).reshape(1)

    def swap_pairs(first, second):
        return (
            lax.ppermute(first, "dom", first_pairs),
            lax.ppermute(second, "dom", second_pairs),
        )

    def exchange(to_next, to_previous):
        first, second = swap_pairs(
            jnp.where(even, to_next, to_previous), jnp.where(even, to_previous, to_next)
        )
        return jnp.where(even, second, first), jnp.where(even, first, second)

    all_entries = support.reshape(dom_count, entry_count)
    entry_source = all_entries // cell_count
    entry_cell = all_entries % cell_count
    entry_atom = jnp.arange(entry_count, dtype=jnp.int32) // supp_count

    def slots_of(dom):
        here = (entry_source == dom).astype(jnp.int32)
        rank = jnp.cumsum(here, axis=1) - 1
        hit = here[:, :, None] * (
            rank[:, :, None] == jnp.arange(slot_cap, dtype=jnp.int32)
        ).astype(jnp.int32)
        cell = jnp.sum(hit * entry_cell[:, :, None], axis=1)
        atom = jnp.sum(hit * entry_atom[None, :, None], axis=1)
        return cell, atom

    offsets = (-1, 0, 1)
    slots = [slots_of((my_dom + offset) % dom_count) for offset in offsets]
    own_entries = lax.dynamic_slice_in_dim(all_entries, my_dom, 1, 0)[0]
    own_source = own_entries // cell_count
    positions = jnp.arange(entry_count, dtype=jnp.int32)
    earlier = (own_source[:, None] == own_source[None, :]) & (
        positions[None, :] < positions[:, None]
    )
    own_slot = own_source * slot_cap + jnp.sum(earlier.astype(jnp.int32), axis=1)

    slot_ids = jnp.arange(slot_count, dtype=jnp.int32)
    place = (slot_ids[:, None] == own_slot[None, :]).astype(jnp.int32)
    entry_of = jnp.sum(place * (positions[None, :] + 1), axis=1) - 1
    outgoing = sort_out(entry_of, proj.reshape(entry_count, proj_count, cell_nodes), dom_count)
    outgoing, near_conn = lax.optimization_barrier((outgoing, conn))
    here = lax.all_to_all(outgoing, "dom", split_axis=0, concat_axis=0, tiled=True)
    conn_low, conn_high = exchange(near_conn, near_conn)
    own = wavefn.T

    conn_rows = conn.reshape(cell_count // STEP_CELLS, 1, STEP_CELLS * cell_nodes)
    mats = joined(cell_mats, 4, cell_count // STEP_CELLS)

    def local(state):
        image, *shared = local_part(side, state, conn_rows, mats)
        return image, swap_pairs(*shared)

    low, high = exchange(own[:, node_count - RIM :], own[:, :RIM])
    current = jnp.concatenate([low, own, high], axis=1)
    here, conn_rows, rotation_rows = lax.optimization_barrier((here, conn_rows, rotation_rows))
    values = swap_pairs(here, here)
    node_rows, atom_rows = [], []
    for offset, cells, (cell, atom) in zip(offsets, (conn_low, conn, conn_high), slots):
        node = cells[cell] + offset * node_count
        node_rows.append(node)
        atom_rows.append(jnp.broadcast_to(atom[:, :, None], node.shape))
    node_row = jnp.stack(node_rows, axis=1).reshape(dom_count, 1, -1)
    atom_row = jnp.stack(atom_rows, axis=1).reshape(dom_count, 1, -1)
    inside = (node_row >= 0) & (node_row < node_count + 2 * RIM)
    high_part = jnp.where(inside, node_row // LO, -1)
    low_part = jnp.where(inside, node_row % LO, 0)
    coeffs = first_coeffs(here, atom_row, high_part, low_part, current)
    coeffs, values = lax.optimization_barrier((coeffs, values))

    def swap(block):
        return lax.all_to_all(block, "dom", split_axis=0, concat_axis=0, tiled=True)

    previous = current
    for turn_index in range(DEG):
        last = turn_index == DEG - 1
        arrived = swap(coeffs)
        if turn_index:
            current, previous = finish(*begun, *shared), current
        else:
            table = assemble(
                side, values[0], here, values[1], atom_row, high_part, low_part, current.shape[1]
            )
        coupled = couple(arrived, coupling)
        coupled, current, table, mats = lax.optimization_barrier((coupled, current, table, mats))
        image, shared = local(current)
        weights = swap(coupled)
        args = (table, weights, current, previous, image)
        if last:
            done = settle(
                turn_index, bounds, side, final_turn(turn_index, bounds, *args), *shared
            )
        else:
            part, coeffs = begin(turn_index, bounds, *args)
            begun = (turn_index, bounds, side, *args, part)
            coeffs, shared = lax.optimization_barrier((coeffs, shared))

    beside = lax.ppermute(done, "band", swaps[1])
    across = lax.ppermute(done, "band", swaps[2])
    last = lax.ppermute(across, "band", swaps[1])
    return rotate((done, beside, across, last), rotation_rows)


def solution(mesh):
    in_specs = (
        P("dom", "band"),
        P("dom", None, None),
        P("dom", None),
        P("dom", None, None, None),
        P("dom", None, None),
        P(),
        P(),
        P(None, "band"),
    )
    out_specs = P("dom", "band")
    return jax.shard_map(body, mesh=mesh, in_specs=in_specs, out_specs=out_specs, check_vma=False)
```
